32 devices in a mesh: seq: 16 (over z, y, x), rep: 2 (over core).
Axes of the slice: x: 2, y: 2, z: 4, core: 2. Of those that a mesh axis runs over, the one named last changes fastest.
Arguments:
- tokens: bfloat16 [2, 8192, 768], P('rep', 'seq'), may hold values from -6 to 6
- lengths: int32 [2, 4], P('rep'), may hold values from 1 to 4479, as said below
- w_query: bfloat16 [768, 768], P(('seq', 'rep')), may hold values from -0.21875 to 0.21875
- b_query: bfloat16 [768], P(('seq', 'rep')), may hold values from -1.5 to 1.5
- w_key: bfloat16 [768, 768], P(('seq', 'rep')), may hold values from -0.21875 to 0.21875
- b_key: bfloat16 [768], P(('seq', 'rep')), may hold values from -1.5 to 1.5
- w_value: bfloat16 [768, 768], P(('seq', 'rep')), may hold values from -0.21875 to 0.21875
- b_value: bfloat16 [768], P(('seq', 'rep')), may hold values from -1.5 to 1.5
- w_out: bfloat16 [768, 768], P(('seq', 'rep')), may hold values from -2.5 to 2.5
- b_out: bfloat16 [768], P(('seq', 'rep')), may hold values from -1.5 to 1.5
- gain_attn: bfloat16 [768], P(('seq', 'rep')), may hold values from 0.5 to 1.5
- shift_attn: bfloat16 [768], P(('seq', 'rep')), may hold values from -1.5 to 1.5
- w_inner: bfloat16 [768, 3072], P(('seq', 'rep')), may hold values from -0.21875 to 0.21875
- b_inner: bfloat16 [3072], P(('seq', 'rep')), may hold values from -1.5 to 1.5
- w_outer: bfloat16 [3072, 768], P(('seq', 'rep')), may hold values from -0.109375 to 0.109375
- b_outer: bfloat16 [768], P(('seq', 'rep')), may hold values from -1.5 to 1.5
- gain_ffn: bfloat16 [768], P(('seq', 'rep')), may hold values from 0.5 to 1.5
- shift_ffn: bfloat16 [768], P(('seq', 'rep')), may hold values from -1.5 to 1.5
- projection: bfloat16 [12, 256, 64], replicated, may hold values from -4 to 4
- cotangent: bfloat16 [2, 8192, 768], P('rep', 'seq'), may hold values from -6 to 6
Outputs:
- output: bfloat16 [2, 8192, 768], P('rep', 'seq')
- token_grad: float32 [2, 8192, 768], P('rep', 'seq')
- grad_w_query: float32 [768, 768], P(('seq', 'rep'))
- grad_b_query: float32 [768], P(('seq', 'rep'))
- grad_w_key: float32 [768, 768], P(('seq', 'rep'))
- grad_b_key: float32 [768], P(('seq', 'rep'))
- grad_w_value: float32 [768, 768], P(('seq', 'rep'))
- grad_b_value: float32 [768], P(('seq', 'rep'))
- grad_w_out: float32 [768, 768], P(('seq', 'rep'))
- grad_b_out: float32 [768], P(('seq', 'rep'))
- grad_gain_attn: float32 [768], P(('seq', 'rep'))
- grad_shift_attn: float32 [768], P(('seq', 'rep'))
- grad_w_inner: float32 [768, 3072], P(('seq', 'rep'))
- grad_b_inner: float32 [3072], P(('seq', 'rep'))
- grad_w_outer: float32 [3072, 768], P(('seq', 'rep'))
- grad_b_outer: float32 [768], P(('seq', 'rep'))
- grad_gain_ffn: float32 [768], P(('seq', 'rep'))
- grad_shift_ffn: float32 [768], P(('seq', 'rep'))
The draws below stay inside these ranges and needn't reach their ends.
Inputs may be any that keep to these rules, and one draw needn't show every extreme that they name: In each group the lengths sum to 8192; the first document holds more than half of the group's positions, and in some group it holds exactly 4479.
All inputs are finite; a program needn't handle non-finite values.
Results may differ from the reference program's by a relative error of at most 0.04.
Values may be sent and summed in bfloat16 or wider, within the bound.
No kernel may reach another device: no remote copies, remote signals or barrier semaphores. Data moves between devices by JAX's collectives and lax.ppermute only.
A program may use at most 256 MiB of HBM per device.

```python
import math
import jax
import jax.numpy as jnp
from jax import lax

HEADS = 12
DH = 64
D = 768
FF = 3072
FEATS = 256
TOK_DEV = 512
NDOC = 4
GROUP_TOK = 8192
GROUPS = 2
N_SEQ = 16


def draw_lengths(key, part):
    key = jax.random.fold_in(key, 11)
    keys_list = jax.random.split(key, 3)
    offset_pick = jax.random.randint(keys_list[0], (GROUPS,), 0, TOK_DEV // 2).astype(jnp.int32)
    widest = jax.random.randint(keys_list[2], (), 0, GROUPS).astype(jnp.int32)
    group_slots = jnp.arange(GROUPS, dtype=jnp.int32)
    offset_pick = jnp.where(group_slots == widest, TOK_DEV // 2 - 1, offset_pick).astype(jnp.int32)
    long_length = GROUP_TOK // 2 + TOK_DEV // 4 + offset_pick
    remain_total = GROUP_TOK - long_length
    rest_count = NDOC - 1
    weights = jax.random.randint(keys_list[1], (GROUPS, rest_count), 2, 5).astype(jnp.int32)
    whole = jnp.sum(weights, axis=1)
    pieces = 1 + (remain_total - rest_count)[:, None] * weights // whole[:, None]
    leftover = remain_total - jnp.sum(pieces, axis=1)
    slots = jnp.arange(rest_count, dtype=jnp.int32)[None, :]
    pieces = pieces + jnp.where(slots == rest_count - 1, leftover[:, None], 0)
    return jnp.concatenate([long_length[:, None], pieces], axis=1).astype(jnp.int32)


def level_of(rng, dims, shards, smallest, top_value):
    def one(dim, shards_of):
        draws = jax.random.uniform(jax.random.fold_in(jax.random.fold_in(rng, 6), dim), (shards_of,), jnp.float32, smallest / len(shards), top_value / len(shards))
        return jnp.repeat(jnp.exp(draws), dims[dim] // shards_of).reshape((-1,) + (1,) * (len(dims) - dim - 1))

    factor_of = one(*shards[0])
    for cut in shards[1:]:
        factor_of = factor_of * one(*cut)
    return factor_of


def scatter_about(key, dims, scale, most, cuts=(), held_as=jnp.bfloat16):
    level = level_of(key, dims, cuts, -0.22, 0.18) if cuts else 1.0
    values = jax.random.normal(key, dims, jnp.float32) * scale * level
    return jnp.minimum(jnp.maximum(values, -most), most).astype(held_as)


def setup_inputs(seed: int = 0) -> dict:
    key_of = jax.random.split(jax.random.key(seed), 21)
    return {
        "tokens": scatter_about(key_of[0], (GROUPS, GROUP_TOK, D), 1.0, 6.0, ((0, 2), (1, 16))),
        "lengths": draw_lengths(jax.random.fold_in(key_of[20], 71), 0),
        "w_query": scatter_about(key_of[2], (D, D), D ** -0.5, 0.21875, ((0, 32),)),
        "b_query": scatter_about(key_of[3], (D,), 0.3, 1.5, ((0, 32),)),
        "w_key": scatter_about(key_of[4], (D, D), D ** -0.5, 0.21875, ((0, 32),)),
        "b_key": scatter_about(key_of[5], (D,), 0.3, 1.5, ((0, 32),)),
        "w_value": scatter_about(key_of[6], (D, D), D ** -0.5, 0.21875, ((0, 32),)),
        "b_value": scatter_about(key_of[7], (D,), 0.3, 1.5, ((0, 32),)),
        "w_out": scatter_about(key_of[8], (D, D), (D // 128) ** -0.5, 2.5, ((0, 32),)),
        "b_out": scatter_about(key_of[9], (D,), 0.3, 1.5, ((0, 32),)),
        "gain_attn": jnp.clip(1.0 + 0.1 * jax.random.normal(key_of[10], (D,), jnp.float32), 0.5, 1.5).astype(jnp.bfloat16),
        "shift_attn": scatter_about(key_of[11], (D,), 0.3, 1.5, ((0, 32),)),
        "w_inner": scatter_about(key_of[12], (D, FF), D ** -0.5, 0.21875, ((0, 32),)),
        "b_inner": scatter_about(key_of[13], (FF,), 0.3, 1.5, ((0, 32),)),
        "w_outer": scatter_about(key_of[14], (FF, D), FF ** -0.5, 0.109375, ((0, 32),)),
        "b_outer": scatter_about(key_of[15], (D,), 0.3, 1.5, ((0, 32),)),
        "gain_ffn": jnp.clip(1.0 + 0.1 * jax.random.normal(key_of[16], (D,), jnp.float32), 0.5, 1.5).astype(jnp.bfloat16),
        "shift_ffn": scatter_about(key_of[17], (D,), 0.3, 1.5, ((0, 32),)),
        "projection": scatter_about(key_of[18], (HEADS, FEATS, DH), 1.0, 4.0),
        "cotangent": scatter_about(key_of[19], (GROUPS, GROUP_TOK, D), 1.0, 6.0, ((0, 2), (1, 16))),
    }


precise = lax.Precision.HIGHEST
norm_eps = 1e-06

@jax.custom_vjp
def low(v):
    return lax.optimization_barrier(v.astype(jnp.bfloat16)).astype(jnp.float32)

@jax.custom_vjp
def low_back(v):
    return v

def low_keep(v):
    return (low(v), None)

def low_pass(kept, grad):
    return (grad,)

def back_keep(v):
    return (v, None)

def back_low(kept, grad):
    return (low(grad),)
low.defvjp(low_keep, low_pass)
low_back.defvjp(back_keep, back_low)

def rounded(value):
    return low(low_back(value))

def layer_norm(value, gain, shift):
    centre = lax.optimization_barrier(jnp.mean(value, axis=-1, keepdims=True))
    centred = value - centre
    spread = lax.optimization_barrier(jnp.mean(centred * centred, axis=-1, keepdims=True))
    return centred * lax.rsqrt(spread + norm_eps) * gain + shift

def gelu_exact(value):
    return jax.nn.gelu(value, approximate=False)

def feature_map(inner_raw, head_rows):
    scale = head_rows.shape[-1] ** (-0.25)
    square = lax.optimization_barrier(jnp.sum(head_rows * head_rows, axis=-1, keepdims=True))
    return jnp.exp(scale * inner_raw - 0.5 * scale * scale * square) / math.sqrt(inner_raw.shape[-1])

def layout(lengths):
    starts = (jnp.cumsum(lengths, axis=1) - lengths).astype(jnp.int32)
    places = jnp.arange(GROUP_TOK, dtype=jnp.int32)
    below = starts[:, None, :] <= places[None, :, None]
    begins = lax.optimization_barrier(jnp.max(jnp.where(below, starts[:, None, :], -1), axis=2))
    doc_ids = lax.optimization_barrier(jnp.sum(below.astype(jnp.int32), axis=2)) - 1
    block_first = places // TOK_DEV * TOK_DEV
    carried = (begins < block_first[None, :]).astype(jnp.float32)
    block_shape = (GROUPS, N_SEQ, TOK_DEV)
    doc_blocks = doc_ids.reshape(block_shape)
    last_rows = (doc_blocks == doc_blocks[:, :, -1:]).astype(jnp.float32)
    block_starts = block_first.reshape(N_SEQ, TOK_DEV)[:, 0]
    flags = (begins.reshape(block_shape)[:, :, -1] >= block_starts[None, :]).astype(jnp.float32)
    return (carried.reshape(block_shape), doc_blocks, last_rows, flags)

def chain_block(carry_in, block_in):
    phi_query, phi_key, values, doc_ids, carried, last_rows, flag_now = block_in
    state_sum, norm_sum = carry_in
    within = jnp.arange(phi_query.shape[0], dtype=jnp.int32)
    allowed = (doc_ids[:, None] == doc_ids[None, :]) & (within[None, :] <= within[:, None])
    scores = jnp.einsum('ihm,jhm->hij', phi_query, phi_key, precision=precise) * allowed.astype(phi_query.dtype)[None]
    scores = low_back(scores)
    numerator = jnp.einsum('hij,jhe->ihe', low(scores), values, precision=precise)
    numerator = numerator + carried[:, None, None] * jnp.einsum('ihm,hme->ihe', phi_query, state_sum, precision=precise)
    denominator = jnp.transpose(lax.optimization_barrier(jnp.sum(scores, axis=2))) + carried[:, None] * jnp.einsum('ihm,hm->ih', phi_query, norm_sum, precision=precise)
    attended = low(low_back(numerator) / denominator[:, :, None])
    passing = 1.0 - flag_now
    new_state = jnp.einsum('jhm,jhe->hme', phi_key * last_rows[:, None, None], values, precision=precise) + passing * state_sum
    new_norm = jnp.einsum('jhm,j->hm', phi_key, last_rows, precision=precise) + passing * norm_sum
    return ((new_state, new_norm), attended)

def forward(tokens_f, weights, projection_f, layout_parts):
    w_query, b_query, w_key, b_key, w_value, b_value, w_out, b_out, gain_attn, shift_attn, w_inner, b_inner, w_outer, b_outer, gain_ffn, shift_ffn = weights
    carried, doc_blocks, last_rows, flags = layout_parts
    model_width = tokens_f.shape[2]
    flat_rows = tokens_f.reshape(GROUPS * GROUP_TOK, model_width)

    def project(weight, bias_row):
        return rounded(jnp.dot(flat_rows, weight, precision=precise) + bias_row).reshape(-1, HEADS, DH)
    queries = project(w_query, b_query)
    keys_all = project(w_key, b_key)
    values = project(w_value, b_value)

    def featurize(head_rows):
        inner_raw = low_back(jnp.einsum('rhe,hme->rhm', head_rows, projection_f, precision=precise))
        return low(feature_map(inner_raw, head_rows))

    def chained(stacked):
        return jnp.swapaxes(stacked.reshape((GROUPS, N_SEQ, TOK_DEV) + stacked.shape[1:]), 0, 1)
    blocks_in = (chained(featurize(queries)), chained(featurize(keys_all)), chained(values), jnp.swapaxes(doc_blocks, 0, 1), jnp.swapaxes(carried, 0, 1), jnp.swapaxes(last_rows, 0, 1), jnp.swapaxes(flags, 0, 1))
    start_state = (jnp.zeros((GROUPS, HEADS, FEATS, DH), jnp.float32), jnp.zeros((GROUPS, HEADS, FEATS), jnp.float32))
    final_state, attended = lax.scan(jax.checkpoint(jax.vmap(chain_block)), start_state, blocks_in)
    attended = jnp.swapaxes(attended, 0, 1).reshape(GROUPS * GROUP_TOK, model_width)
    attn_out = low_back(jnp.dot(attended, w_out, precision=precise) + b_out)
    normed = layer_norm(flat_rows + attn_out, gain_attn, shift_attn)
    hidden_pre = low_back(jnp.dot(low(normed), w_inner, precision=precise) + b_inner)
    activated = low(gelu_exact(hidden_pre))
    ffn_out = low_back(jnp.dot(activated, w_outer, precision=precise) + b_outer)
    result = layer_norm(normed + ffn_out, gain_ffn, shift_ffn)
    return result.reshape(GROUPS, GROUP_TOK, model_width)

def reference(tokens, lengths, w_query, b_query, w_key, b_key, w_value, b_value, w_out, b_out, gain_attn, shift_attn, w_inner, b_inner, w_outer, b_outer, gain_ffn, shift_ffn, projection, cotangent):
    layout_parts = layout(lengths)
    params = (w_query, b_query, w_key, b_key, w_value, b_value, w_out, b_out, gain_attn, shift_attn, w_inner, b_inner, w_outer, b_outer, gain_ffn, shift_ffn)
    params_f = tuple((item.astype(jnp.float32) for item in params))
    projection_f = projection.astype(jnp.float32)

    def wrapped(tokens_f, weights):
        return forward(tokens_f, weights, projection_f, layout_parts)
    result, pull_back = jax.vjp(wrapped, tokens.astype(jnp.float32), params_f)
    grad_tokens, grads = pull_back(cotangent.astype(jnp.float32))
    return (result.astype(jnp.bfloat16), grad_tokens, grads[0], grads[1], grads[2], grads[3], grads[4], grads[5], grads[6], grads[7], grads[8], grads[9], grads[10], grads[11], grads[12], grads[13], grads[14], grads[15])
```

```python
import functools

import jax
import jax.numpy as jnp
from jax import lax
from jax.experimental import pallas as pl
from jax.experimental.pallas import tpu as pltpu
from jax.sharding import PartitionSpec as P

EPS = 1e-06
BF = jnp.bfloat16
F32 = jnp.float32
BOTH = ("seq", "rep")
VMEM_LIMIT = 50 * 1024 * 1024
STATE_ROWS = 16


def dot(a, b):
    return lax.dot_general(a, b, (((1,), (0,)), ((), ())), preferred_element_type=F32)


def dot_nt(a, b):
    return lax.dot_general(a, b, (((1,), (1,)), ((), ())), preferred_element_type=F32)


def dot_tn(a, b):
    return lax.dot_general(a, b, (((0,), (0,)), ((), ())), preferred_element_type=F32)


def half_masks(rows):
    lane = lax.broadcasted_iota(jnp.int32, (rows, 128), 1)
    return (lane < 64, lane >= 64)


def with_ones(values_pair, mask):
    zero = jnp.zeros_like(values_pair)
    return jnp.concatenate(
        [jnp.where(mask, values_pair, zero), jnp.where(mask, zero + 1, zero)], axis=1
    )


def state_matrix(state_ref, head, side, spread):
    state = state_ref[head * 64 : (head + 1) * 64, :]
    norm = state_ref[256:272, :][head : head + 1, :]
    zero = jnp.zeros((64, 256), BF)
    if spread:
        norm_rows = jnp.broadcast_to(norm, (64, 256))
    else:
        row = lax.broadcasted_iota(jnp.int32, (64, 256), 0)
        norm_rows = jnp.where(row == 0, jnp.broadcast_to(norm, (64, 256)), zero)
    if side == 0:
        return jnp.concatenate([state, zero, norm_rows, zero], axis=0)
    return jnp.concatenate([zero, state, zero, norm_rows], axis=0)


def attend_kernel(
    x_ref, wq_ref, wk_ref, wv_ref, bq_ref, bk_ref, bv_ref, pp_ref, mask_ref, last_ref,
    q_ref, k_ref, v_ref, phiq_ref, phik_ref, s_ref, nd_ref, st_ref,
):
    x = x_ref[...]
    rows = x.shape[0]
    half = rows // 2
    scale = 64 ** (-0.25)
    q_ref[...] = (dot(x, wq_ref[...]) + bq_ref[...]).astype(BF)
    k_ref[...] = (dot(x, wk_ref[...]) + bk_ref[...]).astype(BF)
    v_ref[...] = (dot(x, wv_ref[...]) + bv_ref[...]).astype(BF)
    masks = half_masks(rows)
    norms = []
    for pair in range(2):
        lanes = slice(pair * 128, (pair + 1) * 128)
        qp = q_ref[:, lanes]
        kp = k_ref[:, lanes]
        vp = v_ref[:, lanes]
        q2 = qp.astype(F32) * qp.astype(F32)
        k2 = kp.astype(F32) * kp.astype(F32)
        top = jnp.zeros((half, 256), F32)
        bottom = jnp.zeros((half, 256), F32)
        for side in range(2):
            head = 2 * pair + side
            mask = masks[side]
            cols = slice(head * 256, (head + 1) * 256)

            def feature(rows_bf, squares):
                inner = dot(rows_bf, pp_ref[head])
                square = jnp.sum(jnp.where(mask, squares, 0.0), axis=1, keepdims=True)
                return (jnp.exp(scale * inner - square * 0.0625) * 0.0625).astype(BF)

            phi_q = feature(qp, q2)
            phi_k = feature(kp, k2)
            phiq_ref[:, cols] = phi_q
            phik_ref[:, cols] = phi_k
            va = with_ones(vp, mask)
            s_top = (dot_nt(phi_q[:half], phi_k[:half]) * mask_ref[:half, :half]).astype(BF)
            s_bot = (dot_nt(phi_q[half:], phi_k) * mask_ref[half:, :]).astype(BF)
            s_ref[head, :half, :half] = s_top
            s_ref[head, half:, :] = s_bot
            top = top + dot(s_top, va[:half])
            bottom = bottom + dot(s_bot, va)
            state = dot_tn(va, phi_k * last_ref[...])
            st_ref[head * 64 : (head + 1) * 64, :] = state[side * 64 : (side + 1) * 64].astype(BF)
            norms.append(state[128 + side * 64 : 129 + side * 64])
        nd_ref[:half, pair * 256 : (pair + 1) * 256] = top
        nd_ref[half:, pair * 256 : (pair + 1) * 256] = bottom
    norms.append(jnp.zeros((STATE_ROWS - 4, 256), F32))
    st_ref[256:272, :] = jnp.concatenate(norms, axis=0).astype(BF)


def finish_kernel(phiq_ref, nd_ref, cs_ref, car_ref, att_ref, rden_ref):
    car = car_ref[...]
    for pair in range(2):
        nd = nd_ref[:, pair * 256 : (pair + 1) * 256]
        for side in range(2):
            head = 2 * pair + side
            phi_q = phiq_ref[:, head * 256 : (head + 1) * 256] * car
            nd = nd + dot_nt(phi_q, state_matrix(cs_ref, head, side, True))
        rden = 1.0 / nd[:, 128:]
        lanes = slice(pair * 128, (pair + 1) * 128)
        att_ref[:, lanes] = (nd[:, :128] * rden).astype(BF)
        rden_ref[:, lanes] = rden


def state_grad_kernel(ag_ref, rden_ref, att_ref, phiq_ref, car_ref, ng_ref, sg_ref):
    car = car_ref[...]
    norms = []
    for pair in range(2):
        lanes = slice(pair * 128, (pair + 1) * 128)
        ng = ag_ref[:, lanes] * rden_ref[:, lanes]
        dg = -(ng * att_ref[:, lanes].astype(F32))
        both = jnp.concatenate([ng.astype(BF), dg.astype(BF)], axis=1)
        ng_ref[:, pair * 256 : (pair + 1) * 256] = both
        both = both * car
        for side in range(2):
            head = 2 * pair + side
            state = dot_tn(both, phiq_ref[:, head * 256 : (head + 1) * 256])
            sg_ref[head * 64 : (head + 1) * 64, :] = state[side * 64 : (side + 1) * 64].astype(BF)
            tail = state[128 + side * 64 : 192 + side * 64]
            norms.append(jnp.sum(tail, axis=0, keepdims=True))
    norms.append(jnp.zeros((STATE_ROWS - 4, 256), F32))
    sg_ref[256:272, :] = jnp.concatenate(norms, axis=0).astype(BF)


def query_side_kernel(
    ng_ref, v_ref, q_ref, phiq_ref, phik_ref, s_ref, cs_ref, pa_ref, mask_ref, car_ref,
    qg_ref, pk_ref, vg_ref,
):
    rows = q_ref.shape[0]
    half = rows // 2
    scale = 64 ** (-0.25)
    masks = half_masks(rows)
    car = car_ref[...]
    for pair in range(2):
        lanes = slice(pair * 128, (pair + 1) * 128)
        both = ng_ref[:, pair * 256 : (pair + 1) * 256]
        both_car = both * car
        vp = v_ref[:, lanes]
        ng = both[:, :128]
        out_q = jnp.zeros((rows, 256), F32)
        vg_top = jnp.zeros((half, 128), F32)
        vg_bot = jnp.zeros((half, 128), F32)
        for side in range(2):
            head = 2 * pair + side
            cols = slice(head * 256, (head + 1) * 256)
            va = with_ones(vp, masks[side])
            phi_q = phiq_ref[:, cols]
            phi_k = phik_ref[:, cols]
            g_top = (dot_nt(both[:half], va[:half]) * mask_ref[:half, :half]).astype(BF)
            g_bot = (dot_nt(both[half:], va) * mask_ref[half:, :]).astype(BF)
            carry = dot(both_car, state_matrix(cs_ref, head, side, True))
            pq_top = dot(g_top, phi_k[:half]) + carry[:half]
            pq_bot = dot(g_bot, phi_k) + carry[half:]
            pq = jnp.concatenate([pq_top, pq_bot], axis=0)
            iq = (scale * (pq * phi_q.astype(F32))).astype(BF)
            out_q = out_q + dot(iq, pa_ref[head])
            pk = dot_tn(g_bot, phi_q[half:])
            pk_ref[half:, cols] = pk[half:]
            pk_ref[:half, cols] = pk[:half] + dot_tn(g_top, phi_q[:half])
            ngm = jnp.where(masks[side], ng, jnp.zeros_like(ng))
            s_bot = s_ref[head, half:, :]
            s_top = s_ref[head, :half, :half]
            from_bot = dot_tn(s_bot, ngm[half:])
            vg_bot = vg_bot + from_bot[half:]
            vg_top = vg_top + from_bot[:half] + dot_tn(s_top, ngm[:half])
        qp = q_ref[:, lanes].astype(F32)
        qg_ref[:, lanes] = (out_q[:, :128] - scale * qp * out_q[:, 128:]).astype(BF)
        vg_ref[:half, lanes] = vg_top
        vg_ref[half:, lanes] = vg_bot


def key_side_kernel(v_ref, k_ref, phik_ref, ls_ref, pk_ref, vgl_ref, pa_ref, last_ref, kg_ref, vg_ref):
    rows = k_ref.shape[0]
    scale = 64 ** (-0.25)
    masks = half_masks(rows)
    last = last_ref[...]
    for pair in range(2):
        lanes = slice(pair * 128, (pair + 1) * 128)
        vp = v_ref[:, lanes]
        out_k = jnp.zeros((rows, 256), F32)
        vg = vgl_ref[:, lanes]
        for side in range(2):
            head = 2 * pair + side
            cols = slice(head * 256, (head + 1) * 256)
            va = with_ones(vp, masks[side]) * last
            phi_k = phik_ref[:, cols]
            later = state_matrix(ls_ref, head, side, False)
            pk = pk_ref[:, cols] + dot(va, later)
            ik = (scale * (pk * phi_k.astype(F32))).astype(BF)
            out_k = out_k + dot(ik, pa_ref[head])
            vg = vg + dot_nt(phi_k * last, later[:128])
        kp = k_ref[:, lanes].astype(F32)
        kg_ref[:, lanes] = (out_k[:, :128] - scale * kp * out_k[:, 128:]).astype(BF)
        vg_ref[:, lanes] = vg.astype(BF)


def columns(rows, width):
    return pl.BlockSpec((rows, width), lambda g: (0, g))


def whole(*shape):
    return pl.BlockSpec(shape, lambda g: (0,) * len(shape))


def leading(count, *rest):
    return pl.BlockSpec((count,) + rest, lambda g: (g,) + (0,) * len(rest))


def call(kernel, groups, in_specs, out_specs, outs, args, flops=0, moved=0):
    return pl.pallas_call(
        kernel,
        grid=(groups,),
        in_specs=in_specs,
        out_specs=out_specs,
        out_shape=[jax.ShapeDtypeStruct(shape, kind) for shape, kind in outs],
        compiler_params=pltpu.CompilerParams(vmem_limit_bytes=VMEM_LIMIT),
        cost_estimate=pl.CostEstimate(flops=flops, bytes_accessed=moved, transcendentals=0),
    )(*args)


def exchange(state, matrix):
    count = lax.axis_size("seq")
    rows, width = state.shape
    extra = -rows % count
    if extra:
        state = jnp.pad(state, ((0, extra), (0, 0)))
    parts = state.reshape(count, (rows + extra) // count, width)
    parts = lax.all_to_all(parts, "seq", 0, 0)
    summed = jnp.einsum("cb,bre->cre", matrix.astype(BF), parts, preferred_element_type=F32)
    back = lax.all_to_all(summed.astype(BF), "seq", 0, 0)
    return back.reshape(rows + extra, width)[:rows]


def norm_rows(value):
    centre = jnp.mean(value, axis=-1, keepdims=True)
    centred = value - centre
    spread = jnp.mean(centred * centred, axis=-1, keepdims=True)
    inverse = lax.rsqrt(spread + EPS)
    return centred * inverse, inverse


def norm_back(grad, gain, unit, inverse):
    scaled = grad * gain
    mean_one = jnp.mean(scaled, axis=-1, keepdims=True)
    mean_two = jnp.mean(scaled * unit, axis=-1, keepdims=True)
    return (scaled - mean_one - unit * mean_two) * inverse


def local(
    tokens, lengths, w_query, b_query, w_key, b_key, w_value, b_value, w_out, b_out,
    gain_attn, shift_attn, w_inner, b_inner, w_outer, b_outer, gain_ffn, shift_ffn,
    projection, cotangent,
):
    rows = tokens.shape[1]
    width = tokens.shape[2]
    heads = projection.shape[0]
    feats = projection.shape[1]
    groups = heads // 4
    blocks = lax.axis_size("seq")
    devices = blocks * lax.axis_size("rep")
    here = lax.axis_index("seq")
    share = w_query.shape[0]
    hidden_width = w_inner.shape[1]
    parts = hidden_width // width

    bias_list = (
        b_query, b_key, b_value, b_out, gain_attn, shift_attn, b_inner, b_outer, gain_ffn, shift_ffn,
    )
    bias_flat = jnp.concatenate(bias_list)
    packed_rows = share * (4 + 2 * parts)
    total_rows = -(-(packed_rows + 1) // 8) * 8
    bias_block = jnp.pad(
        bias_flat[None], ((0, total_rows - packed_rows - 1), (0, width - bias_flat.shape[0]))
    )
    packed = jnp.concatenate(
        [w_query, w_key, w_value, w_out]
        + [w_inner[:, j * width : (j + 1) * width] for j in range(parts)]
        + [w_outer, bias_block],
        axis=0,
    )
    everything = lax.all_gather(packed, BOTH, axis=0, tiled=True).reshape(devices, total_rows, width)

    def matrix_at(first, count):
        return everything[:, first : first + count].reshape(devices * count, width)

    wq, wk, wv, wo = (matrix_at(i * share, share) for i in range(4))
    w_in = [matrix_at((4 + j) * share, share) for j in range(parts)]
    w_in = jnp.concatenate(w_in, axis=1)
    w_ou = matrix_at((4 + parts) * share, parts * share)
    bias_all = everything[:, packed_rows, :]
    vectors = []
    at = 0
    for item in bias_list:
        size = item.shape[0]
        vectors.append(bias_all[:, at : at + size].reshape(1, devices * size).astype(F32))
        at += size
    bq, bk, bv, bo, ga, sa, bi, bu, gf, sf = vectors

    sizes = lengths[0]
    starts = jnp.cumsum(sizes) - sizes

    def begin_of(places):
        below = starts[None, :] <= places[:, None]
        begins = jnp.max(jnp.where(below, starts[None, :], -1), axis=1)
        return begins, jnp.sum(below.astype(jnp.int32), axis=1) - 1

    offset = here * rows
    places = offset + jnp.arange(rows, dtype=jnp.int32)
    begins, docs = begin_of(places)
    carried = (begins < offset).astype(BF)
    last = (docs == docs[-1]).astype(BF)
    causal = (docs[:, None] == docs[None, :]) & (places[None, :] <= places[:, None])
    mask = causal.astype(F32)
    car = jnp.broadcast_to(carried[:, None], (rows, 256))
    las = jnp.broadcast_to(last[:, None], (rows, 256))
    block = jnp.arange(blocks, dtype=jnp.int32)
    end_begin, _ = begin_of(block * rows + rows - 1)
    flags = (end_begin >= block * rows).astype(jnp.int32)
    before = jnp.cumsum(flags) - flags
    reach = (block[:, None] > block[None, :]) & (
        before[:, None] - before[None, :] - flags[None, :] == 0
    )
    reach = reach.astype(BF)

    pairs = projection.reshape(heads // 2, 2, feats, 64)
    first = jnp.pad(pairs[:, 0], ((0, 0), (0, 0), (0, 64)))
    second = jnp.pad(pairs[:, 1], ((0, 0), (0, 0), (64, 0)))
    padded = jnp.stack([first, second], axis=1).reshape(heads, feats, 128)
    lane = jnp.arange(128)
    lane_ones = jnp.stack([lane < 64, lane >= 64]).astype(BF)
    lane_ones = jnp.broadcast_to(lane_ones[None, :, None, :], (heads // 2, 2, feats, 128))
    pa = jnp.concatenate([padded, lane_ones.reshape(heads, feats, 128)], axis=-1)
    pp = jnp.swapaxes(padded, 1, 2)

    x = tokens[0]
    srows = 256 + STATE_ROWS
    w4 = 4 * feats
    queries, keys, values, phi_q, phi_k, scores, nd, state = call(
        attend_kernel, groups,
        [
            whole(rows, width), columns(width, 256), columns(width, 256), columns(width, 256),
            columns(1, 256), columns(1, 256), columns(1, 256), leading(4, 128, feats),
            whole(rows, rows), whole(rows, 256),
        ],
        [
            columns(rows, 256), columns(rows, 256), columns(rows, 256), columns(rows, w4),
            columns(rows, w4), leading(4, rows, rows), columns(rows, 512), leading(srows, 256),
        ],
        [
            ((rows, width), BF), ((rows, width), BF), ((rows, width), BF),
            ((rows, heads * feats), BF), ((rows, heads * feats), BF), ((heads, rows, rows), BF),
            ((rows, 2 * width), F32), ((groups * srows, 256), BF),
        ],
        (x, wq, wk, wv, bq, bk, bv, pp, mask, las),
        flops=12_000_000_000, moved=30_000_000,
    )
    carry = exchange(state, reach)
    attended, rden = call(
        finish_kernel, groups,
        [columns(rows, w4), columns(rows, 512), leading(srows, 256), whole(rows, 256)],
        [columns(rows, 256), columns(rows, 256)],
        [((rows, width), BF), ((rows, width), F32)],
        (phi_q, nd, carry, car),
        flops=1_000_000_000, moved=10_000_000,
    )

    xf = x.astype(F32)
    unit_one, inv_one = norm_rows(xf + dot(attended, wo) + bo)
    normed = unit_one * ga + sa
    normed_bf = normed.astype(BF)
    hidden = dot(normed_bf, w_in) + bi
    cdf = 0.5 * (1.0 + lax.erf(hidden * (0.5**0.5)))
    activated = (hidden * cdf).astype(BF)
    ffn = dot(activated, w_ou) + bu
    unit_two, inv_two = norm_rows(normed + ffn)
    output = (unit_two * gf + sf).astype(BF)

    upstream = cotangent[0].astype(F32)
    sum_grad = norm_back(upstream, gf, unit_two, inv_two)
    g_gf = jnp.sum(upstream * unit_two, axis=0)
    g_sf = jnp.sum(upstream, axis=0)
    ffn_grad = sum_grad.astype(BF)
    g_bu = jnp.sum(ffn_grad.astype(F32), axis=0)
    density = jnp.exp(-0.5 * hidden * hidden) * 0.3989422804014327
    hidden_grad = (dot_nt(ffn_grad, w_ou) * (cdf + hidden * density)).astype(BF)
    g_bi = jnp.sum(hidden_grad.astype(F32), axis=0)
    normed_grad = sum_grad + dot_nt(hidden_grad, w_in)
    first_grad = norm_back(normed_grad, ga, unit_one, inv_one)
    g_ga = jnp.sum(normed_grad * unit_one, axis=0)
    g_sa = jnp.sum(normed_grad, axis=0)
    attn_grad = first_grad.astype(BF)
    g_bo = jnp.sum(attn_grad.astype(F32), axis=0)
    attended_grad = dot_nt(attn_grad, wo)
    g_wu = dot_tn(activated, ffn_grad).astype(BF)
    g_wi = [
        dot_tn(normed_bf, hidden_grad[:, j * width : (j + 1) * width]).astype(BF)
        for j in range(parts)
    ]
    g_wo = dot_tn(attended, attn_grad).astype(BF)

    ng, state_back = call(
        state_grad_kernel, groups,
        [columns(rows, 256), columns(rows, 256), columns(rows, 256), columns(rows, w4), whole(rows, 256)],
        [columns(rows, 512), leading(srows, 256)],
        [((rows, 2 * width), BF), ((groups * srows, 256), BF)],
        (attended_grad, rden, attended, phi_q, car),
        flops=1_000_000_000, moved=10_000_000,
    )
    later = exchange(state_back, reach.T)
    query_grad, pk_local, vg_local = call(
        query_side_kernel, groups,
        [
            columns(rows, 512), columns(rows, 256), columns(rows, 256), columns(rows, w4),
            columns(rows, w4), leading(4, rows, rows), leading(srows, 256), leading(4, feats, 256),
            whole(rows, rows), whole(rows, 256),
        ],
        [columns(rows, 256), columns(rows, w4), columns(rows, 256)],
        [((rows, width), BF), ((rows, heads * feats), F32), ((rows, width), F32)],
        (ng, values, queries, phi_q, phi_k, scores, carry, pa, mask, car),
        flops=12_000_000_000, moved=30_000_000,
    )
    key_grad, value_grad = call(
        key_side_kernel, groups,
        [
            columns(rows, 256), columns(rows, 256), columns(rows, w4), leading(srows, 256),
            columns(rows, w4), columns(rows, 256), leading(4, feats, 256), whole(rows, 256),
        ],
        [columns(rows, 256), columns(rows, 256)],
        [((rows, width), BF), ((rows, width), BF)],
        (values, keys, phi_k, later, pk_local, vg_local, pa, las),
        flops=3_000_000_000, moved=12_000_000,
    )
    token_grad = (
        first_grad + dot_nt(query_grad, wq) + dot_nt(key_grad, wk) + dot_nt(value_grad, wv)
    )
    g_wq = dot_tn(x, query_grad).astype(BF)
    g_wk = dot_tn(x, key_grad).astype(BF)
    g_wv = dot_tn(x, value_grad).astype(BF)

    def column_sum(value):
        return jnp.sum(value.astype(F32), axis=0)

    g_bq, g_bk, g_bv = column_sum(query_grad), column_sum(key_grad), column_sum(value_grad)
    vector_grads = (g_bq, g_bk, g_bv, g_bo, g_ga, g_sa, g_bi, g_bu, g_gf, g_sf)
    bias_grads = jnp.concatenate([g.reshape(devices, -1) for g in vector_grads], axis=1)
    bias_grads = jnp.pad(
        bias_grads[:, None, :],
        ((0, 0), (0, total_rows - packed_rows - 1), (0, width - bias_grads.shape[1])),
    )
    pieces = [g.reshape(devices, -1, width) for g in [g_wq, g_wk, g_wv, g_wo] + g_wi + [g_wu]]
    send = jnp.concatenate(pieces + [bias_grads.astype(BF)], axis=1)
    got = lax.psum_scatter(send, BOTH, scatter_dimension=0, tiled=False).astype(F32)

    def rows_at(index, count):
        return got[index * share : (index + count) * share]

    bias_row = got[packed_rows]
    vec = []
    at = 0
    for item in bias_list:
        vec.append(bias_row[at : at + item.shape[0]])
        at += item.shape[0]
    grad_inner = jnp.concatenate([rows_at(4 + j, 1) for j in range(parts)], axis=1)
    return (
        output[None], token_grad[None],
        rows_at(0, 1), vec[0], rows_at(1, 1), vec[1], rows_at(2, 1), vec[2], rows_at(3, 1), vec[3],
        vec[4], vec[5], grad_inner, vec[6], rows_at(4 + parts, parts), vec[7], vec[8], vec[9],
    )


def solution(mesh):
    rows2 = P(("seq", "rep"), None)
    vec = P(("seq", "rep"))
    blocks = P("rep", "seq", None)
    in_specs = (
        blocks, P("rep", None), rows2, vec, rows2, vec, rows2, vec, rows2, vec, vec, vec,
        rows2, vec, rows2, vec, vec, vec, P(), blocks,
    )
    out_specs = (
        blocks, blocks, rows2, vec, rows2, vec, rows2, vec, rows2, vec, vec, vec,
        rows2, vec, rows2, vec, vec, vec,
    )
    return jax.shard_map(local, mesh=mesh, in_specs=in_specs, out_specs=out_specs, check_vma=False)
```

```python
import functools

import jax
import jax.numpy as jnp
from jax import lax
from jax.experimental import pallas as pl
from jax.experimental.pallas import tpu as pltpu
from jax.sharding import PartitionSpec as P

EPS = 1e-06
BF = jnp.bfloat16
F32 = jnp.float32
BOTH = ("seq", "rep")
VMEM_LIMIT = 50 * 1024 * 1024
STATE_ROWS = 16


def dot(a, b):
    return lax.dot_general(a, b, (((1,), (0,)), ((), ())), preferred_element_type=F32)


def dot_nt(a, b):
    return lax.dot_general(a, b, (((1,), (1,)), ((), ())), preferred_element_type=F32)


def dot_tn(a, b):
    return lax.dot_general(a, b, (((0,), (0,)), ((), ())), preferred_element_type=F32)


def half_masks(rows):
    lane = lax.broadcasted_iota(jnp.int32, (rows, 128), 1)
    return (lane < 64, lane >= 64)


def with_ones(values_pair, mask):
    zero = jnp.zeros_like(values_pair)
    return jnp.concatenate(
        [jnp.where(mask, values_pair, zero), jnp.where(mask, zero + 1, zero)], axis=1
    )


def state_matrix(state_ref, head, side, spread):
    state = state_ref[head * 64 : (head + 1) * 64, :]
    norm = state_ref[256:272, :][head : head + 1, :]
    zero = jnp.zeros((64, 256), BF)
    if spread:
        norm_rows = jnp.broadcast_to(norm, (64, 256))
    else:
        row = lax.broadcasted_iota(jnp.int32, (64, 256), 0)
        norm_rows = jnp.where(row == 0, jnp.broadcast_to(norm, (64, 256)), zero)
    if side == 0:
        return jnp.concatenate([state, zero, norm_rows, zero], axis=0)
    return jnp.concatenate([zero, state, zero, norm_rows], axis=0)


def features(rows_bf, squares, mask, padded):
    scale = 64 ** (-0.25)
    square = jnp.sum(jnp.where(mask, squares, 0.0), axis=1, keepdims=True)
    return (jnp.exp(scale * dot(rows_bf, padded) - square * 0.0625) * 0.0625).astype(BF)


def keys_kernel(
    x_ref, wk_ref, wv_ref, bk_ref, bv_ref, pp_ref, last_ref, k_ref, v_ref, phik_ref, st_ref
):
    x = x_ref[...]
    k_ref[...] = (dot(x, wk_ref[...]) + bk_ref[...]).astype(BF)
    v_ref[...] = (dot(x, wv_ref[...]) + bv_ref[...]).astype(BF)
    masks = half_masks(x.shape[0])
    norms = []
    for pair in range(2):
        lanes = slice(pair * 128, (pair + 1) * 128)
        kp = k_ref[:, lanes]
        vp = v_ref[:, lanes]
        k2 = kp.astype(F32) * kp.astype(F32)
        for side in range(2):
            head = 2 * pair + side
            phi_k = features(kp, k2, masks[side], pp_ref[head])
            phik_ref[:, head * 256 : (head + 1) * 256] = phi_k
            state = dot_tn(with_ones(vp, masks[side]), phi_k * last_ref[...])
            st_ref[head * 64 : (head + 1) * 64, :] = state[side * 64 : (side + 1) * 64].astype(BF)
            norms.append(state[128 + side * 64 : 129 + side * 64])
    norms.append(jnp.zeros((STATE_ROWS - 4, 256), F32))
    st_ref[256:272, :] = jnp.concatenate(norms, axis=0).astype(BF)


def queries_kernel(
    x_ref, wq_ref, bq_ref, v_ref, phik_ref, pp_ref, mask_ref, q_ref, phiq_ref, s_ref, nd_ref
):
    x = x_ref[...]
    rows = x.shape[0]
    half = rows // 2
    q_ref[...] = (dot(x, wq_ref[...]) + bq_ref[...]).astype(BF)
    masks = half_masks(rows)
    for pair in range(2):
        lanes = slice(pair * 128, (pair + 1) * 128)
        qp = q_ref[:, lanes]
        vp = v_ref[:, lanes]
        q2 = qp.astype(F32) * qp.astype(F32)
        top = jnp.zeros((half, 256), F32)
        bottom = jnp.zeros((half, 256), F32)
        for side in range(2):
            head = 2 * pair + side
            cols = slice(head * 256, (head + 1) * 256)
            phi_q = features(qp, q2, masks[side], pp_ref[head])
            phi_k = phik_ref[:, cols]
            phiq_ref[:, cols] = phi_q
            va = with_ones(vp, masks[side])
            s_top = (dot_nt(phi_q[:half], phi_k[:half]) * mask_ref[:half, :half]).astype(BF)
            s_bot = (dot_nt(phi_q[half:], phi_k) * mask_ref[half:, :]).astype(BF)
            s_ref[head, :half, :half] = s_top
            s_ref[head, half:, :] = s_bot
            top = top + dot(s_top, va[:half])
            bottom = bottom + dot(s_bot, va)
        nd_ref[:half, pair * 256 : (pair + 1) * 256] = top
        nd_ref[half:, pair * 256 : (pair + 1) * 256] = bottom


def finish_kernel(phiq_ref, nd_ref, cs_ref, car_ref, att_ref, rden_ref):
    car = car_ref[...]
    for pair in range(2):
        nd = nd_ref[:, pair * 256 : (pair + 1) * 256]
        for side in range(2):
            head = 2 * pair + side
            phi_q = phiq_ref[:, head * 256 : (head + 1) * 256] * car
            nd = nd + dot_nt(phi_q, state_matrix(cs_ref, head, side, True))
        rden = 1.0 / nd[:, 128:]
        lanes = slice(pair * 128, (pair + 1) * 128)
        att_ref[:, lanes] = (nd[:, :128] * rden).astype(BF)
        rden_ref[:, lanes] = rden


def state_grad_kernel(ag_ref, rden_ref, att_ref, phiq_ref, car_ref, ng_ref, sg_ref):
    car = car_ref[...]
    norms = []
    for pair in range(2):
        lanes = slice(pair * 128, (pair + 1) * 128)
        ng = ag_ref[:, lanes] * rden_ref[:, lanes]
        dg = -(ng * att_ref[:, lanes].astype(F32))
        both = jnp.concatenate([ng.astype(BF), dg.astype(BF)], axis=1)
        ng_ref[:, pair * 256 : (pair + 1) * 256] = both
        both = both * car
        for side in range(2):
            head = 2 * pair + side
            state = dot_tn(both, phiq_ref[:, head * 256 : (head + 1) * 256])
            sg_ref[head * 64 : (head + 1) * 64, :] = state[side * 64 : (side + 1) * 64].astype(BF)
            tail = state[128 + side * 64 : 192 + side * 64]
            norms.append(jnp.sum(tail, axis=0, keepdims=True))
    norms.append(jnp.zeros((STATE_ROWS - 4, 256), F32))
    sg_ref[256:272, :] = jnp.concatenate(norms, axis=0).astype(BF)


def query_side_kernel(
    ng_ref, v_ref, q_ref, phiq_ref, phik_ref, s_ref, cs_ref, pa_ref, mask_ref, car_ref,
    qg_ref, pk_ref, vg_ref,
):
    rows = q_ref.shape[0]
    half = rows // 2
    scale = 64 ** (-0.25)
    masks = half_masks(rows)
    car = car_ref[...]
    for pair in range(2):
        lanes = slice(pair * 128, (pair + 1) * 128)
        both = ng_ref[:, pair * 256 : (pair + 1) * 256]
        both_car = both * car
        vp = v_ref[:, lanes]
        ng = both[:, :128]
        out_q = jnp.zeros((rows, 256), F32)
        vg_top = jnp.zeros((half, 128), F32)
        vg_bot = jnp.zeros((half, 128), F32)
        for side in range(2):
            head = 2 * pair + side
            cols = slice(head * 256, (head + 1) * 256)
            va = with_ones(vp, masks[side])
            phi_q = phiq_ref[:, cols]
            phi_k = phik_ref[:, cols]
            g_top = (dot_nt(both[:half], va[:half]) * mask_ref[:half, :half]).astype(BF)
            g_bot = (dot_nt(both[half:], va) * mask_ref[half:, :]).astype(BF)
            carry = dot(both_car, state_matrix(cs_ref, head, side, True))
            pq_top = dot(g_top, phi_k[:half]) + carry[:half]
            pq_bot = dot(g_bot, phi_k) + carry[half:]
            pq = jnp.concatenate([pq_top, pq_bot], axis=0)
            iq = (scale * (pq * phi_q.astype(F32))).astype(BF)
            out_q = out_q + dot(iq, pa_ref[head])
            pk = dot_tn(g_bot, phi_q[half:])
            pk_ref[half:, cols] = pk[half:]
            pk_ref[:half, cols] = pk[:half] + dot_tn(g_top, phi_q[:half])
            ngm = jnp.where(masks[side], ng, jnp.zeros_like(ng))
            s_bot = s_ref[head, half:, :]
            s_top = s_ref[head, :half, :half]
            from_bot = dot_tn(s_bot, ngm[half:])
            vg_bot = vg_bot + from_bot[half:]
            vg_top = vg_top + from_bot[:half] + dot_tn(s_top, ngm[:half])
        qp = q_ref[:, lanes].astype(F32)
        qg_ref[:, lanes] = (out_q[:, :128] - scale * qp * out_q[:, 128:]).astype(BF)
        vg_ref[:half, lanes] = vg_top
        vg_ref[half:, lanes] = vg_bot


def key_side_kernel(v_ref, k_ref, phik_ref, ls_ref, pk_ref, vgl_ref, pa_ref, last_ref, kg_ref, vg_ref):
    rows = k_ref.shape[0]
    scale = 64 ** (-0.25)
    masks = half_masks(rows)
    last = last_ref[...]
    for pair in range(2):
        lanes = slice(pair * 128, (pair + 1) * 128)
        vp = v_ref[:, lanes]
        out_k = jnp.zeros((rows, 256), F32)
        vg = vgl_ref[:, lanes]
        for side in range(2):
            head = 2 * pair + side
            cols = slice(head * 256, (head + 1) * 256)
            va = with_ones(vp, masks[side]) * last
            phi_k = phik_ref[:, cols]
            later = state_matrix(ls_ref, head, side, False)
            pk = pk_ref[:, cols] + dot(va, later)
            ik = (scale * (pk * phi_k.astype(F32))).astype(BF)
            out_k = out_k + dot(ik, pa_ref[head])
            vg = vg + dot_nt(phi_k * last, later[:128])
        kp = k_ref[:, lanes].astype(F32)
        kg_ref[:, lanes] = (out_k[:, :128] - scale * kp * out_k[:, 128:]).astype(BF)
        vg_ref[:, lanes] = vg.astype(BF)


def columns(rows, width, first=0):
    return pl.BlockSpec((rows, width), lambda g: (0, g + first))


def whole(*shape):
    return pl.BlockSpec(shape, lambda g: (0,) * len(shape))


def leading(count, *rest):
    return pl.BlockSpec((count,) + rest, lambda g: (g,) + (0,) * len(rest))


def call(kernel, groups, in_specs, out_specs, outs, args, flops=0, moved=0):
    return pl.pallas_call(
        kernel,
        grid=(groups,),
        in_specs=in_specs,
        out_specs=out_specs,
        out_shape=[jax.ShapeDtypeStruct(shape, kind) for shape, kind in outs],
        compiler_params=pltpu.CompilerParams(vmem_limit_bytes=VMEM_LIMIT),
        cost_estimate=pl.CostEstimate(flops=flops, bytes_accessed=moved, transcendentals=0),
    )(*args)


def exchange(state, matrix):
    count = lax.axis_size("seq")
    rows, width = state.shape
    extra = -rows % count
    if extra:
        state = jnp.pad(state, ((0, extra), (0, 0)))
    parts = state.reshape(count, (rows + extra) // count, width)
    parts = lax.all_to_all(parts, "seq", 0, 0)
    summed = jnp.einsum("cb,bre->cre", matrix.astype(BF), parts, preferred_element_type=F32)

    def end(sums):
        back = lax.all_to_all(sums, "seq", 0, 0)
        return back.reshape(rows + extra, width)[:rows]

    return summed.astype(BF), end


def device_bits():
    count = lax.axis_size("seq") * lax.axis_size("rep")
    bits = count.bit_length() - 1
    assert count == 1 << bits and bits >= 3
    return count, bits, lax.axis_index("seq") * lax.axis_size("rep") + lax.axis_index("rep")


def swap(value, bit):
    count, _, _ = device_bits()
    return lax.ppermute(value, BOTH, [(i, i ^ (1 << bit)) for i in range(count)])


def gather_pairs(block):
    _, bits, me = device_bits()
    rows, width = block.shape

    def grow(held, bit, axis):
        other = swap(held, bit)
        low = (me >> bit) & 1 == 0
        return jnp.stack([jnp.where(low, held, other), jnp.where(low, other, held)], axis=axis)

    held = block[None]
    for bit in range(bits - 1, 2, -1):
        held = grow(held, bit, 1).reshape(-1, rows, width)
    half = width // 256 * 128
    one, two = held[:, :, :half], held[:, :, half:]
    one = grow(grow(one, 2, 1), 1, 2).reshape(-1, rows, half)
    two = grow(grow(two, 1, 1), 2, 1).reshape(-1, rows, width - half)
    return grow(jnp.concatenate([one, two], axis=2), 0, 1).reshape(-1, width)


class PairScatter:
    def __init__(self, pieces):
        count, self.bits, self.me = device_bits()
        pairs = [piece.reshape(count // 2, 2, -1, piece.shape[-1]) for piece in pieces]
        mine = jnp.concatenate([self.pick(piece, 0, 1, True) for piece in pairs], axis=2)
        other = jnp.concatenate([self.pick(piece, 0, 1, False) for piece in pairs], axis=2)
        lanes = mine.shape[2]
        half = lanes // 256 * 128
        rest = tuple(range(3, self.bits))
        self.orders = [(1, 2) + rest, (2, 1) + rest]
        self.left = [list(range(self.bits - 1, 0, -1)) for _ in self.orders]
        self.held = []
        for part in (slice(0, half), slice(half, lanes)):
            held = self.add(mine[:, :, part], swap(other[:, :, part], 0))
            self.held.append(held.reshape((2,) * (self.bits - 1) + held.shape[1:]))

    def pick(self, value, bit, axis, own):
        index = (self.me >> bit) & 1
        return lax.dynamic_index_in_dim(value, index if own else 1 - index, axis, False)

    def add(self, mine, other):
        return (mine.astype(F32) + other.astype(F32)).astype(BF)

    def step(self):
        for k, order in enumerate(self.orders):
            bit, self.orders[k] = order[0], order[1:]
            axis = self.left[k].index(bit)
            self.left[k].remove(bit)
            held = self.held[k]
            moved = swap(self.pick(held, bit, axis, False), bit)
            self.held[k] = self.add(self.pick(held, bit, axis, True), moved)

    def after(self, value):
        self.me, value = lax.optimization_barrier((self.me, value))
        return value

    def finish(self):
        while self.orders[0]:
            self.step()
        return jnp.concatenate(self.held, axis=1).astype(F32)


def columns_of(vectors, count):
    rows = min(v.size for v in vectors) // count
    found = [jnp.swapaxes(v.reshape(count, -1, rows), 1, 2) for v in vectors]
    found = jnp.concatenate(found, axis=2)
    return jnp.pad(found, ((0, 0), (0, 0), (0, 128 - found.shape[2])))


def vectors_of(block, sizes, count):
    rows = block.shape[0] // count
    found = []
    at = 0
    for size in sizes:
        lanes = size // rows
        item = block[:, at : at + lanes].reshape(count, rows, lanes)
        found.append(jnp.swapaxes(item, 1, 2).reshape(1, -1).astype(F32))
        at += lanes
    return found


def norm_rows(value):
    centre = jnp.mean(value, axis=-1, keepdims=True)
    centred = value - centre
    spread = jnp.mean(centred * centred, axis=-1, keepdims=True)
    inverse = lax.rsqrt(spread + EPS)
    return centred * inverse, inverse


def norm_back(grad, gain, unit, inverse):
    scaled = grad * gain
    mean_one = jnp.mean(scaled, axis=-1, keepdims=True)
    mean_two = jnp.mean(scaled * unit, axis=-1, keepdims=True)
    return (scaled - mean_one - unit * mean_two) * inverse


def local(
    tokens, lengths, w_query, b_query, w_key, b_key, w_value, b_value, w_out, b_out,
    gain_attn, shift_attn, w_inner, b_inner, w_outer, b_outer, gain_ffn, shift_ffn,
    projection, cotangent,
):
    rows = tokens.shape[1]
    width = tokens.shape[2]
    heads = projection.shape[0]
    feats = projection.shape[1]
    groups = heads // 4
    blocks = lax.axis_size("seq")
    devices = blocks * lax.axis_size("rep")
    here = lax.axis_index("seq")
    share = w_query.shape[0]
    hidden_width = w_inner.shape[1]
    parts = hidden_width // width

    first_vectors = (b_query, b_key, b_value)
    rest_vectors = (b_out, gain_attn, shift_attn, b_inner, b_outer, gain_ffn, shift_ffn)
    pack_one = jnp.concatenate([w_query, w_key, w_value, columns_of(first_vectors, 1)[0]], axis=1)
    pack_two = jnp.concatenate([w_out, w_inner, columns_of(rest_vectors, 1)[0]], axis=1)
    all_two = lax.all_gather(pack_two, BOTH, axis=0, tiled=True)
    w_ou = lax.all_gather(w_outer, BOTH, axis=0, tiled=True)
    all_one = gather_pairs(pack_one)
    bq, bk, bv = vectors_of(all_one[:, 3 * width :], [v.shape[0] for v in first_vectors], devices)
    wo = all_two[:, :width]
    w_in = all_two[:, width : width + hidden_width]
    bo, ga, sa, bi, bu, gf, sf = vectors_of(
        all_two[:, width + hidden_width :], [v.shape[0] for v in rest_vectors], devices
    )

    def shares(value):
        return value.reshape(devices, -1, width)

    sizes = lengths[0]
    starts = jnp.cumsum(sizes) - sizes

    def begin_of(places):
        below = starts[None, :] <= places[:, None]
        begins = jnp.max(jnp.where(below, starts[None, :], -1), axis=1)
        return begins, jnp.sum(below.astype(jnp.int32), axis=1) - 1

    offset = here * rows
    places = offset + jnp.arange(rows, dtype=jnp.int32)
    begins, docs = begin_of(places)
    carried = (begins < offset).astype(BF)
    last = (docs == docs[-1]).astype(BF)
    causal = (docs[:, None] == docs[None, :]) & (places[None, :] <= places[:, None])
    mask = causal.astype(F32)
    car = jnp.broadcast_to(carried[:, None], (rows, 256))
    las = jnp.broadcast_to(last[:, None], (rows, 256))
    block = jnp.arange(blocks, dtype=jnp.int32)
    end_begin, _ = begin_of(block * rows + rows - 1)
    flags = (end_begin >= block * rows).astype(jnp.int32)
    before = jnp.cumsum(flags) - flags
    reach = (block[:, None] > block[None, :]) & (
        before[:, None] - before[None, :] - flags[None, :] == 0
    )
    reach = reach.astype(BF)

    pairs = projection.reshape(heads // 2, 2, feats, 64)
    first = jnp.pad(pairs[:, 0], ((0, 0), (0, 0), (0, 64)))
    second = jnp.pad(pairs[:, 1], ((0, 0), (0, 0), (64, 0)))
    padded = jnp.stack([first, second], axis=1).reshape(heads, feats, 128)
    lane = jnp.arange(128)
    lane_ones = jnp.stack([lane < 64, lane >= 64]).astype(BF)
    lane_ones = jnp.broadcast_to(lane_ones[None, :, None, :], (heads // 2, 2, feats, 128))
    pa = jnp.concatenate([padded, lane_ones.reshape(heads, feats, 128)], axis=-1)
    pp = jnp.swapaxes(padded, 1, 2)

    x = tokens[0]
    srows = 256 + STATE_ROWS
    w4 = 4 * feats
    keys, values, phi_k, state = call(
        keys_kernel, groups,
        [
            whole(rows, width), columns(width, 256, groups), columns(width, 256, 2 * groups),
            columns(1, 256), columns(1, 256), leading(4, 128, feats), whole(rows, 256),
        ],
        [columns(rows, 256), columns(rows, 256), columns(rows, w4), leading(srows, 256)],
        [
            ((rows, width), BF), ((rows, width), BF), ((rows, heads * feats), BF),
            ((groups * srows, 256), BF),
        ],
        (x, all_one, all_one, bk, bv, pp, las),
        flops=4_000_000_000, moved=9_000_000,
    )
    sums, end = exchange(state, reach)
    queries, phi_q, scores, nd = call(
        queries_kernel, groups,
        [
            whole(rows, width), columns(width, 256), columns(1, 256), columns(rows, 256),
            columns(rows, w4), leading(4, 128, feats), whole(rows, rows),
        ],
        [columns(rows, 256), columns(rows, w4), leading(4, rows, rows), columns(rows, 512)],
        [
            ((rows, width), BF), ((rows, heads * feats), BF), ((heads, rows, rows), BF),
            ((rows, 2 * width), F32),
        ],
        (x, all_one, bq, values, phi_k, pp, mask),
        flops=8_000_000_000, moved=20_000_000,
    )
    sums, nd = lax.optimization_barrier((sums, nd))
    carry = end(sums)
    attended, rden = call(
        finish_kernel, groups,
        [columns(rows, w4), columns(rows, 512), leading(srows, 256), whole(rows, 256)],
        [columns(rows, 256), columns(rows, 256)],
        [((rows, width), BF), ((rows, width), F32)],
        (phi_q, nd, carry, car),
        flops=1_000_000_000, moved=10_000_000,
    )

    xf = x.astype(F32)
    unit_one, inv_one = norm_rows(xf + dot(attended, wo) + bo)
    normed = unit_one * ga + sa
    normed_bf = normed.astype(BF)
    hidden = dot(normed_bf, w_in) + bi
    cdf = 0.5 * (1.0 + lax.erf(hidden * (0.5**0.5)))
    activated = (hidden * cdf).astype(BF)
    ffn = dot(activated, w_ou) + bu
    unit_two, inv_two = norm_rows(normed + ffn)
    output = (unit_two * gf + sf).astype(BF)

    upstream = cotangent[0].astype(F32)
    sum_grad = norm_back(upstream, gf, unit_two, inv_two)
    g_gf = jnp.sum(upstream * unit_two, axis=0)
    g_sf = jnp.sum(upstream, axis=0)
    ffn_grad = sum_grad.astype(BF)
    g_bu = jnp.sum(ffn_grad.astype(F32), axis=0)
    g_wu = dot_tn(activated, ffn_grad).astype(BF)
    density = jnp.exp(-0.5 * hidden * hidden) * 0.3989422804014327
    hidden_grad = (dot_nt(ffn_grad, w_ou) * (cdf + hidden * density)).astype(BF)
    g_bi = jnp.sum(hidden_grad.astype(F32), axis=0)

    def inner_grads(first, count, grad):
        return [
            dot_tn(normed_bf, grad[:, j * width : (j + 1) * width]).astype(BF)
            for j in range(first, first + count)
        ]

    early = parts // 2
    sent = [shares(g) for g in inner_grads(0, early, hidden_grad) + [g_wu]]
    got_ffn = lax.psum_scatter(
        jnp.concatenate(sent, axis=1), BOTH, scatter_dimension=0, tiled=False
    ).astype(F32)
    normed_grad = sum_grad + dot_nt(hidden_grad, w_in)
    first_grad = norm_back(normed_grad, ga, unit_one, inv_one)
    g_ga = jnp.sum(normed_grad * unit_one, axis=0)
    g_sa = jnp.sum(normed_grad, axis=0)
    attn_grad = first_grad.astype(BF)
    g_bo = jnp.sum(attn_grad.astype(F32), axis=0)
    attended_grad = dot_nt(attn_grad, wo)

    ng, state_back = call(
        state_grad_kernel, groups,
        [columns(rows, 256), columns(rows, 256), columns(rows, 256), columns(rows, w4), whole(rows, 256)],
        [columns(rows, 512), leading(srows, 256)],
        [((rows, 2 * width), BF), ((groups * srows, 256), BF)],
        (attended_grad, rden, attended, phi_q, car),
        flops=1_000_000_000, moved=10_000_000,
    )
    sums, end = exchange(state_back, reach.T)
    query_grad, pk_local, vg_local = call(
        query_side_kernel, groups,
        [
            columns(rows, 512), columns(rows, 256), columns(rows, 256), columns(rows, w4),
            columns(rows, w4), leading(4, rows, rows), leading(srows, 256), leading(4, feats, 256),
            whole(rows, rows), whole(rows, 256),
        ],
        [columns(rows, 256), columns(rows, w4), columns(rows, 256)],
        [((rows, width), BF), ((rows, heads * feats), F32), ((rows, width), F32)],
        (ng, values, queries, phi_q, phi_k, scores, carry, pa, mask, car),
        flops=12_000_000_000, moved=30_000_000,
    )
    sums, query_grad, hidden_late, attn_late = lax.optimization_barrier(
        (sums, query_grad, hidden_grad, attn_grad)
    )
    later = end(sums)
    g_wo = dot_tn(attended, attn_late).astype(BF)
    g_wi = dot_tn(normed_bf, hidden_late[:, early * width :]).astype(BF)
    key_grad, value_grad = call(
        key_side_kernel, groups,
        [
            columns(rows, 256), columns(rows, 256), columns(rows, w4), leading(srows, 256),
            columns(rows, w4), columns(rows, 256), leading(4, feats, 256), whole(rows, 256),
        ],
        [columns(rows, 256), columns(rows, 256)],
        [((rows, width), BF), ((rows, width), BF)],
        (values, keys, phi_k, later, pk_local, vg_local, pa, las),
        flops=3_000_000_000, moved=12_000_000,
    )
    qkv_grad = jnp.concatenate([query_grad, key_grad, value_grad], axis=1)
    token_grad = first_grad + dot_nt(qkv_grad, all_one[:, : 3 * width])
    g_qkv = dot_tn(x, qkv_grad).astype(BF)
    column_grads = columns_of(
        [jnp.sum(qkv_grad[:, i * width : (i + 1) * width].astype(F32), axis=0) for i in range(3)]
        + [g_bo, g_ga, g_sa, g_bi, g_bu, g_gf, g_sf],
        devices,
    )

    def side_by_side(value):
        return value.reshape(devices, share, -1)

    late = [side_by_side(g) for g in (g_wo, g_wi, g_qkv)] + [column_grads.astype(BF)]
    chain = PairScatter(late)
    chain.step()
    got_ffn = chain.after(got_ffn)
    got = chain.finish()
    late_lanes = g_wi.shape[1]
    at = width + late_lanes
    grad_inner = jnp.concatenate(
        [got_ffn[j * share : (j + 1) * share] for j in range(early)] + [got[:, width:at]], axis=1
    )
    o_bq, o_bk, o_bv, o_bo, o_ga, o_sa, o_bi, o_bu, o_gf, o_sf = (
        v[0]
        for v in vectors_of(
            got[:, at + 3 * width :], [v.shape[0] for v in first_vectors + rest_vectors], 1
        )
    )
    return (
        output[None], token_grad[None],
        got[:, at : at + width], o_bq, got[:, at + width : at + 2 * width], o_bk,
        got[:, at + 2 * width : at + 3 * width], o_bv,
        got[:, :width], o_bo, o_ga, o_sa, grad_inner, o_bi,
        got_ffn[early * share :], o_bu, o_gf, o_sf,
    )


def solution(mesh):
    rows2 = P(("seq", "rep"), None)
    vec = P(("seq", "rep"))
    blocks = P("rep", "seq", None)
    in_specs = (
        blocks, P("rep", None), rows2, vec, rows2, vec, rows2, vec, rows2, vec, vec, vec,
        rows2, vec, rows2, vec, vec, vec, P(), blocks,
    )
    out_specs = (
        blocks, blocks, rows2, vec, rows2, vec, rows2, vec, rows2, vec, vec, vec,
        rows2, vec, rows2, vec, vec, vec,
    )
    return jax.shard_map(local, mesh=mesh, in_specs=in_specs, out_specs=out_specs, check_vma=False)
```

```python
import functools

import jax
import jax.numpy as jnp
from jax import lax
from jax.experimental import pallas as pl
from jax.experimental.pallas import tpu as pltpu
from jax.sharding import PartitionSpec as P

EPS = 1e-06
BF = jnp.bfloat16
F32 = jnp.float32
BOTH = ("seq", "rep")
VMEM_LIMIT = 50 * 1024 * 1024
STATE_ROWS = 16


def dot(a, b):
    return lax.dot_general(a, b, (((1,), (0,)), ((), ())), preferred_element_type=F32)


def dot_nt(a, b):
    return lax.dot_general(a, b, (((1,), (1,)), ((), ())), preferred_element_type=F32)


def dot_tn(a, b):
    return lax.dot_general(a, b, (((0,), (0,)), ((), ())), preferred_element_type=F32)


def half_masks(rows):
    lane = lax.broadcasted_iota(jnp.int32, (rows, 128), 1)
    return (lane < 64, lane >= 64)


def with_ones(values_pair, mask):
    zero = jnp.zeros_like(values_pair)
    return jnp.concatenate(
        [jnp.where(mask, values_pair, zero), jnp.where(mask, zero + 1, zero)], axis=1
    )


def state_matrix(state_ref, head, side, spread):
    state = state_ref[head * 64 : (head + 1) * 64, :]
    norm = state_ref[256:272, :][head : head + 1, :]
    zero = jnp.zeros((64, 256), BF)
    if spread:
        norm_rows = jnp.broadcast_to(norm, (64, 256))
    else:
        row = lax.broadcasted_iota(jnp.int32, (64, 256), 0)
        norm_rows = jnp.where(row == 0, jnp.broadcast_to(norm, (64, 256)), zero)
    if side == 0:
        return jnp.concatenate([state, zero, norm_rows, zero], axis=0)
    return jnp.concatenate([zero, state, zero, norm_rows], axis=0)


def features(rows_bf, squares, mask, padded):
    scale = 64 ** (-0.25)
    square = jnp.sum(jnp.where(mask, squares, 0.0), axis=1, keepdims=True)
    return (jnp.exp(scale * dot(rows_bf, padded) - square * 0.0625) * 0.0625).astype(BF)


def keys_kernel(
    x_ref, wk_ref, wv_ref, bk_ref, bv_ref, pp_ref, last_ref, k_ref, v_ref, phik_ref, st_ref
):
    x = x_ref[...]
    k_ref[...] = (dot(x, wk_ref[...]) + bk_ref[...]).astype(BF)
    v_ref[...] = (dot(x, wv_ref[...]) + bv_ref[...]).astype(BF)
    masks = half_masks(x.shape[0])
    norms = []
    for pair in range(2):
        lanes = slice(pair * 128, (pair + 1) * 128)
        kp = k_ref[:, lanes]
        vp = v_ref[:, lanes]
        k2 = kp.astype(F32) * kp.astype(F32)
        for side in range(2):
            head = 2 * pair + side
            phi_k = features(kp, k2, masks[side], pp_ref[head])
            phik_ref[:, head * 256 : (head + 1) * 256] = phi_k
            state = dot_tn(with_ones(vp, masks[side]), phi_k * last_ref[...])
            st_ref[head * 64 : (head + 1) * 64, :] = state[side * 64 : (side + 1) * 64].astype(BF)
            norms.append(state[128 + side * 64 : 129 + side * 64])
    norms.append(jnp.zeros((STATE_ROWS - 4, 256), F32))
    st_ref[256:272, :] = jnp.concatenate(norms, axis=0).astype(BF)


def queries_kernel(
    x_ref, wq_ref, bq_ref, v_ref, phik_ref, pp_ref, mask_ref, q_ref, phiq_ref, s_ref, nd_ref
):
    x = x_ref[...]
    rows = x.shape[0]
    half = rows // 2
    q_ref[...] = (dot(x, wq_ref[...]) + bq_ref[...]).astype(BF)
    masks = half_masks(rows)
    for pair in range(2):
        lanes = slice(pair * 128, (pair + 1) * 128)
        qp = q_ref[:, lanes]
        vp = v_ref[:, lanes]
        q2 = qp.astype(F32) * qp.astype(F32)
        top = jnp.zeros((half, 256), F32)
        bottom = jnp.zeros((half, 256), F32)
        for side in range(2):
            head = 2 * pair + side
            cols = slice(head * 256, (head + 1) * 256)
            phi_q = features(qp, q2, masks[side], pp_ref[head])
            phi_k = phik_ref[:, cols]
            phiq_ref[:, cols] = phi_q
            va = with_ones(vp, masks[side])
            s_top = (dot_nt(phi_q[:half], phi_k[:half]) * mask_ref[:half, :half]).astype(BF)
            s_bot = (dot_nt(phi_q[half:], phi_k) * mask_ref[half:, :]).astype(BF)
            s_ref[head, :half, :half] = s_top
            s_ref[head, half:, :] = s_bot
            top = top + dot(s_top, va[:half])
            bottom = bottom + dot(s_bot, va)
        nd_ref[:half, pair * 256 : (pair + 1) * 256] = top
        nd_ref[half:, pair * 256 : (pair + 1) * 256] = bottom


def finish_kernel(phiq_ref, nd_ref, cs_ref, car_ref, att_ref, rden_ref):
    car = car_ref[...]
    for pair in range(2):
        nd = nd_ref[:, pair * 256 : (pair + 1) * 256]
        for side in range(2):
            head = 2 * pair + side
            phi_q = phiq_ref[:, head * 256 : (head + 1) * 256] * car
            nd = nd + dot_nt(phi_q, state_matrix(cs_ref, head, side, True))
        rden = 1.0 / nd[:, 128:]
        lanes = slice(pair * 128, (pair + 1) * 128)
        att_ref[:, lanes] = (nd[:, :128] * rden).astype(BF)
        rden_ref[:, lanes] = rden


def state_grad_kernel(ag_ref, rden_ref, att_ref, phiq_ref, car_ref, _send, ng_ref, sg_ref):
    car = car_ref[...]
    norms = []
    for pair in range(2):
        lanes = slice(pair * 128, (pair + 1) * 128)
        ng = ag_ref[:, lanes] * rden_ref[:, lanes]
        dg = -(ng * att_ref[:, lanes].astype(F32))
        both = jnp.concatenate([ng.astype(BF), dg.astype(BF)], axis=1)
        ng_ref[:, pair * 256 : (pair + 1) * 256] = both
        both = both * car
        for side in range(2):
            head = 2 * pair + side
            state = dot_tn(both, phiq_ref[:, head * 256 : (head + 1) * 256])
            sg_ref[head * 64 : (head + 1) * 64, :] = state[side * 64 : (side + 1) * 64].astype(BF)
            tail = state[128 + side * 64 : 192 + side * 64]
            norms.append(jnp.sum(tail, axis=0, keepdims=True))
    norms.append(jnp.zeros((STATE_ROWS - 4, 256), F32))
    sg_ref[256:272, :] = jnp.concatenate(norms, axis=0).astype(BF)


def query_side_kernel(
    ng_ref, v_ref, q_ref, phiq_ref, phik_ref, s_ref, cs_ref, pa_ref, mask_ref, car_ref,
    qg_ref, pk_ref, vg_ref,
):
    rows = q_ref.shape[0]
    half = rows // 2
    scale = 64 ** (-0.25)
    masks = half_masks(rows)
    car = car_ref[...]
    for pair in range(2):
        lanes = slice(pair * 128, (pair + 1) * 128)
        both = ng_ref[:, pair * 256 : (pair + 1) * 256]
        both_car = both * car
        vp = v_ref[:, lanes]
        ng = both[:, :128]
        out_q = jnp.zeros((rows, 256), F32)
        vg_top = jnp.zeros((half, 128), F32)
        vg_bot = jnp.zeros((half, 128), F32)
        for side in range(2):
            head = 2 * pair + side
            cols = slice(head * 256, (head + 1) * 256)
            va = with_ones(vp, masks[side])
            phi_q = phiq_ref[:, cols]
            phi_k = phik_ref[:, cols]
            g_top = (dot_nt(both[:half], va[:half]) * mask_ref[:half, :half]).astype(BF)
            g_bot = (dot_nt(both[half:], va) * mask_ref[half:, :]).astype(BF)
            carry = dot(both_car, state_matrix(cs_ref, head, side, True))
            pq_top = dot(g_top, phi_k[:half]) + carry[:half]
            pq_bot = dot(g_bot, phi_k) + carry[half:]
            pq = jnp.concatenate([pq_top, pq_bot], axis=0)
            iq = (scale * (pq * phi_q.astype(F32))).astype(BF)
            out_q = out_q + dot(iq, pa_ref[head])
            pk = dot_tn(g_bot, phi_q[half:])
            pk_ref[half:, cols] = pk[half:]
            pk_ref[:half, cols] = pk[:half] + dot_tn(g_top, phi_q[:half])
            ngm = jnp.where(masks[side], ng, jnp.zeros_like(ng))
            s_bot = s_ref[head, half:, :]
            s_top = s_ref[head, :half, :half]
            from_bot = dot_tn(s_bot, ngm[half:])
            vg_bot = vg_bot + from_bot[half:]
            vg_top = vg_top + from_bot[:half] + dot_tn(s_top, ngm[:half])
        qp = q_ref[:, lanes].astype(F32)
        qg_ref[:, lanes] = (out_q[:, :128] - scale * qp * out_q[:, 128:]).astype(BF)
        vg_ref[:half, lanes] = vg_top
        vg_ref[half:, lanes] = vg_bot


def key_side_kernel(
    v_ref, k_ref, phik_ref, ls_ref, pk_ref, vgl_ref, pa_ref, last_ref, kg_ref, vg_ref
):
    rows = k_ref.shape[0]
    scale = 64 ** (-0.25)
    masks = half_masks(rows)
    last = last_ref[...]
    for pair in range(2):
        lanes = slice(pair * 128, (pair + 1) * 128)
        vp = v_ref[:, lanes]
        out_k = jnp.zeros((rows, 256), F32)
        vg = vgl_ref[:, lanes]
        for side in range(2):
            head = 2 * pair + side
            cols = slice(head * 256, (head + 1) * 256)
            va = with_ones(vp, masks[side]) * last
            phi_k = phik_ref[:, cols]
            later = state_matrix(ls_ref, head, side, False)
            pk = pk_ref[:, cols] + dot(va, later)
            ik = (scale * (pk * phi_k.astype(F32))).astype(BF)
            out_k = out_k + dot(ik, pa_ref[head])
            vg = vg + dot_nt(phi_k * last, later[:128])
        kp = k_ref[:, lanes].astype(F32)
        kg_ref[:, lanes] = (out_k[:, :128] - scale * kp * out_k[:, 128:]).astype(BF)
        vg_ref[:, lanes] = vg.astype(BF)


def columns(rows, width, first=0):
    return pl.BlockSpec((rows, width), lambda g: (0, g + first))


def whole(*shape):
    return pl.BlockSpec(shape, lambda g: (0,) * len(shape))


def leading(count, *rest):
    return pl.BlockSpec((count,) + rest, lambda g: (g,) + (0,) * len(rest))


def call(kernel, groups, in_specs, out_specs, outs, args, flops=0, moved=0):
    return pl.pallas_call(
        kernel,
        grid=(groups,),
        in_specs=in_specs,
        out_specs=out_specs,
        out_shape=[jax.ShapeDtypeStruct(shape, kind) for shape, kind in outs],
        compiler_params=pltpu.CompilerParams(vmem_limit_bytes=VMEM_LIMIT),
        cost_estimate=pl.CostEstimate(flops=flops, bytes_accessed=moved, transcendentals=0),
    )(*args)


def exchange(state, matrix):
    count = lax.axis_size("seq")
    rows, width = state.shape
    extra = -rows % count
    if extra:
        state = jnp.pad(state, ((0, extra), (0, 0)))
    parts = state.reshape(count, (rows + extra) // count, width)
    parts = lax.all_to_all(parts, "seq", 0, 0)
    summed = jnp.einsum("cb,bre->cre", matrix.astype(BF), parts, preferred_element_type=F32)

    def end(sums):
        back = lax.all_to_all(sums, "seq", 0, 0)
        return back.reshape(rows + extra, width)[:rows]

    return summed.astype(BF), end


def device_bits():
    count = lax.axis_size("seq") * lax.axis_size("rep")
    bits = count.bit_length() - 1
    assert count == 1 << bits and bits >= 3
    return count, bits, lax.axis_index("seq") * lax.axis_size("rep") + lax.axis_index("rep")


def swap(value, bit):
    count, _, _ = device_bits()
    return lax.ppermute(value, BOTH, [(i, i ^ (1 << bit)) for i in range(count)])


def stage_orders(bits, ways):
    order = list(range(1, bits))
    turned = min(ways, bits - 1)
    return [order[k:turned] + order[:k] + order[turned:] for k in range(turned)]


def gather_pairs(block):
    _, bits, me = device_bits()
    rows, width = block.shape

    def grow(held, bit, axis):
        other = swap(held, bit)
        low = (me >> bit) & 1 == 0
        return jnp.stack([jnp.where(low, held, other), jnp.where(low, other, held)], axis=axis)

    orders = [order[::-1] for order in stage_orders(bits, 3)]
    tiles = width // 128
    cuts = [tiles * k // len(orders) * 128 for k in range(len(orders) + 1)]
    parts = [block[:, cuts[k] : cuts[k + 1]] for k in range(len(orders))]
    have = [[] for _ in orders]
    if len({order[0] for order in orders}) == 1:
        shared = orders[0][0]
        grown = grow(block, shared, 0)
        parts = [grown[:, :, cuts[k] : cuts[k + 1]] for k in range(len(orders))]
        have = [[shared] for _ in orders]
        orders = [order[1:] for order in orders]
    for stage in range(len(orders[0])):
        for k, order in enumerate(orders):
            bit = order[stage]
            axis = sum(b > bit for b in have[k])
            have[k].append(bit)
            parts[k] = grow(parts[k], bit, axis)
    parts = [part.reshape((-1,) + part.shape[-2:]) for part in parts]
    return grow(jnp.concatenate(parts, axis=2), 0, 1).reshape(-1, width)


def add(mine, other):
    return (mine.astype(F32) + other.astype(F32)).astype(BF)


def pick(me, value, bit, axis, own):
    index = (me >> bit) & 1
    return lax.dynamic_index_in_dim(value, index if own else 1 - index, axis, False)


def core_sums(pieces):
    count, _, _ = device_bits()
    cores = lax.axis_size("rep")
    pairs = [piece.reshape(count // 2, 2, -1, piece.shape[-1]) for piece in pieces]
    both = jnp.swapaxes(jnp.concatenate(pairs, axis=3), 0, 1)
    groups = [[core, core + 1] for core in range(0, cores, 2)]
    both = lax.all_to_all(both, "rep", 0, 0, axis_index_groups=groups)
    return add(both[0], both[1])


class PairScatter:
    def __init__(self, value):
        _, self.bits, self.me = device_bits()
        self.orders = stage_orders(self.bits, 3)
        turned = len(self.orders)
        self.left = [list(range(self.bits - 1, 0, -1)) for _ in self.orders]
        tiles = value.shape[2] // 128
        cuts = [tiles * k // turned * 128 for k in range(turned + 1)]
        value = value.reshape((2,) * (self.bits - 1) + value.shape[1:])
        self.held = [value[..., cuts[k] : cuts[k + 1]] for k in range(turned)]

    def step(self):
        for k, order in enumerate(self.orders):
            bit, self.orders[k] = order[0], order[1:]
            axis = self.left[k].index(bit)
            self.left[k].remove(bit)
            held = self.held[k]
            moved = swap(pick(self.me, held, bit, axis, False), bit)
            self.held[k] = add(pick(self.me, held, bit, axis, True), moved)

    def after(self, value):
        self.me, value = lax.optimization_barrier((self.me, value))
        return value


def columns_of(vectors, count):
    rows = min(v.size for v in vectors) // count
    found = [jnp.swapaxes(v.reshape(count, -1, rows), 1, 2) for v in vectors]
    found = jnp.concatenate(found, axis=2)
    return jnp.pad(found, ((0, 0), (0, 0), (0, 128 - found.shape[2])))


def vectors_of(block, sizes, count):
    rows = block.shape[0] // count
    found = []
    at = 0
    for size in sizes:
        lanes = size // rows
        item = block[:, at : at + lanes].reshape(count, rows, lanes)
        found.append(jnp.swapaxes(item, 1, 2).reshape(1, -1).astype(F32))
        at += lanes
    return found


def finish_gradients(held, got_ffn, share, width, early, parts, sizes):
    late = (parts - early) * width
    shapes = [(share, width)] * 4 + [(share, parts * width), (parts * share, width)]
    shapes += [(size // share, share) for size in sizes]

    def pieces(got, ffn, turn):
        at = width + late
        found = [got[:, at + k * width : at + (k + 1) * width] for k in range(3)] + [got[:, :width]]
        early_parts = [ffn[k * share : (k + 1) * share] for k in range(early)]
        found.append(jnp.concatenate(early_parts + [got[:, width:at]], axis=1))
        found.append(ffn[early * share :])
        turned = turn(got[:, at + 3 * width :])
        row = 0
        for size in sizes:
            found.append(turned[row : row + size // share])
            row += size // share
        return found

    if share % 8:
        got = jnp.concatenate(held, axis=1).astype(F32)
        return pieces(got, got_ffn.astype(F32), jnp.transpose)

    def kernel(*refs):
        count = len(held)
        got = jnp.concatenate([ref[...].astype(F32) for ref in refs[:count]], axis=1)
        for ref, value in zip(refs[count + 1 :], pieces(got, refs[count][...].astype(F32), jnp.transpose)):
            ref[...] = value

    return pl.pallas_call(
        kernel,
        out_shape=[jax.ShapeDtypeStruct(shape, F32) for shape in shapes],
        compiler_params=pltpu.CompilerParams(vmem_limit_bytes=VMEM_LIMIT),
        cost_estimate=pl.CostEstimate(flops=1000, bytes_accessed=2_000_000, transcendentals=0),
    )(*held, got_ffn)


def norm_rows(value):
    centre = jnp.mean(value, axis=-1, keepdims=True)
    centred = value - centre
    spread = jnp.mean(centred * centred, axis=-1, keepdims=True)
    inverse = lax.rsqrt(spread + EPS)
    return centred * inverse, inverse


def norm_back(grad, gain, unit, inverse):
    scaled = grad * gain
    mean_one = jnp.mean(scaled, axis=-1, keepdims=True)
    mean_two = jnp.mean(scaled * unit, axis=-1, keepdims=True)
    return (scaled - mean_one - unit * mean_two) * inverse


def local(
    tokens, lengths, w_query, b_query, w_key, b_key, w_value, b_value, w_out, b_out,
    gain_attn, shift_attn, w_inner, b_inner, w_outer, b_outer, gain_ffn, shift_ffn,
    projection, cotangent,
):
    rows = tokens.shape[1]
    width = tokens.shape[2]
    heads = projection.shape[0]
    feats = projection.shape[1]
    groups = heads // 4
    blocks = lax.axis_size("seq")
    devices = blocks * lax.axis_size("rep")
    here = lax.axis_index("seq")
    share = w_query.shape[0]
    hidden_width = w_inner.shape[1]
    parts = hidden_width // width

    first_vectors = (b_query, b_key, b_value)
    rest_vectors = (b_out, gain_attn, shift_attn, b_inner, b_outer, gain_ffn, shift_ffn)
    pack_one = jnp.concatenate([w_query, w_key, w_value, w_out, columns_of(first_vectors, 1)[0]], axis=1)
    pack_two = jnp.concatenate([w_inner, columns_of(rest_vectors, 1)[0]], axis=1)
    all_two = lax.all_gather(pack_two, BOTH, axis=0, tiled=True)
    w_ou = lax.all_gather(w_outer, BOTH, axis=0, tiled=True)
    all_one = gather_pairs(pack_one)
    bq, bk, bv = vectors_of(all_one[:, 4 * width :], [v.shape[0] for v in first_vectors], devices)
    wo = all_one[:, 3 * width : 4 * width]
    w_in = all_two[:, :hidden_width]
    bo, ga, sa, bi, bu, gf, sf = vectors_of(
        all_two[:, hidden_width:], [v.shape[0] for v in rest_vectors], devices
    )

    def shares(value):
        return value.reshape(devices, -1, width)

    sizes = lengths[0]
    starts = jnp.cumsum(sizes) - sizes

    def begin_of(places):
        below = starts[None, :] <= places[:, None]
        begins = jnp.max(jnp.where(below, starts[None, :], -1), axis=1)
        return begins, jnp.sum(below.astype(jnp.int32), axis=1) - 1

    offset = here * rows
    places = offset + jnp.arange(rows, dtype=jnp.int32)
    begins, docs = begin_of(places)
    carried = (begins < offset).astype(BF)
    last = (docs == docs[-1]).astype(BF)
    causal = (docs[:, None] == docs[None, :]) & (places[None, :] <= places[:, None])
    mask = causal.astype(F32)
    car = jnp.broadcast_to(carried[:, None], (rows, 256))
    las = jnp.broadcast_to(last[:, None], (rows, 256))
    block = jnp.arange(blocks, dtype=jnp.int32)
    end_begin, _ = begin_of(block * rows + rows - 1)
    flags = (end_begin >= block * rows).astype(jnp.int32)
    before = jnp.cumsum(flags) - flags
    reach = (block[:, None] > block[None, :]) & (
        before[:, None] - before[None, :] - flags[None, :] == 0
    )
    reach = reach.astype(BF)

    pairs = projection.reshape(heads // 2, 2, feats, 64)
    first = jnp.pad(pairs[:, 0], ((0, 0), (0, 0), (0, 64)))
    second = jnp.pad(pairs[:, 1], ((0, 0), (0, 0), (64, 0)))
    padded = jnp.stack([first, second], axis=1).reshape(heads, feats, 128)
    lane = jnp.arange(128)
    lane_ones = jnp.stack([lane < 64, lane >= 64]).astype(BF)
    lane_ones = jnp.broadcast_to(lane_ones[None, :, None, :], (heads // 2, 2, feats, 128))
    pa = jnp.concatenate([padded, lane_ones.reshape(heads, feats, 128)], axis=-1)
    pp = jnp.swapaxes(padded, 1, 2)

    x = tokens[0]
    srows = 256 + STATE_ROWS
    w4 = 4 * feats
    keys, values, phi_k, state = call(
        keys_kernel, groups,
        [
            whole(rows, width), columns(width, 256, groups), columns(width, 256, 2 * groups),
            columns(1, 256), columns(1, 256), leading(4, 128, feats), whole(rows, 256),
        ],
        [columns(rows, 256), columns(rows, 256), columns(rows, w4), leading(srows, 256)],
        [
            ((rows, width), BF), ((rows, width), BF), ((rows, heads * feats), BF),
            ((groups * srows, 256), BF),
        ],
        (x, all_one, all_one, bk, bv, pp, las),
        flops=4_000_000_000, moved=9_000_000,
    )
    sums, end = exchange(state, reach)
    queries, phi_q, scores, nd = call(
        queries_kernel, groups,
        [
            whole(rows, width), columns(width, 256), columns(1, 256), columns(rows, 256),
            columns(rows, w4), leading(4, 128, feats), whole(rows, rows),
        ],
        [columns(rows, 256), columns(rows, w4), leading(4, rows, rows), columns(rows, 512)],
        [
            ((rows, width), BF), ((rows, heads * feats), BF), ((heads, rows, rows), BF),
            ((rows, 2 * width), F32),
        ],
        (x, all_one, bq, values, phi_k, pp, mask),
        flops=8_000_000_000, moved=20_000_000,
    )
    sums, nd = lax.optimization_barrier((sums, nd))
    carry = end(sums)
    attended, rden = call(
        finish_kernel, groups,
        [columns(rows, w4), columns(rows, 512), leading(srows, 256), whole(rows, 256)],
        [columns(rows, 256), columns(rows, 256)],
        [((rows, width), BF), ((rows, width), F32)],
        (phi_q, nd, carry, car),
        flops=1_000_000_000, moved=10_000_000,
    )

    xf = x.astype(F32)
    unit_one, inv_one = norm_rows(xf + dot(attended, wo) + bo)
    normed = unit_one * ga + sa
    normed_bf = normed.astype(BF)
    hidden = dot(normed_bf, w_in) + bi
    cdf = 0.5 * (1.0 + lax.erf(hidden * (0.5**0.5)))
    activated = (hidden * cdf).astype(BF)
    ffn = dot(activated, w_ou) + bu
    unit_two, inv_two = norm_rows(normed + ffn)
    output = (unit_two * gf + sf).astype(BF)

    upstream = cotangent[0].astype(F32)
    sum_grad = norm_back(upstream, gf, unit_two, inv_two)
    g_gf = jnp.sum(upstream * unit_two, axis=0)
    g_sf = jnp.sum(upstream, axis=0)
    ffn_grad = sum_grad.astype(BF)
    g_bu = jnp.sum(ffn_grad.astype(F32), axis=0)
    g_wu = dot_tn(activated, ffn_grad).astype(BF)
    density = jnp.exp(-0.5 * hidden * hidden) * 0.3989422804014327
    hidden_grad = (dot_nt(ffn_grad, w_ou) * (cdf + hidden * density)).astype(BF)
    g_bi = jnp.sum(hidden_grad.astype(F32), axis=0)

    send = shares(g_wu)
    early = 0
    got_ffn = lax.psum_scatter(send, BOTH, scatter_dimension=0, tiled=False)
    normed_grad = sum_grad + dot_nt(hidden_grad, w_in)
    first_grad = norm_back(normed_grad, ga, unit_one, inv_one)
    g_ga = jnp.sum(normed_grad * unit_one, axis=0)
    g_sa = jnp.sum(normed_grad, axis=0)
    attn_grad = first_grad.astype(BF)
    g_bo = jnp.sum(attn_grad.astype(F32), axis=0)
    attended_grad = dot_nt(attn_grad, wo)

    ng, state_back = call(
        state_grad_kernel, groups,
        [
            columns(rows, 256), columns(rows, 256), columns(rows, 256), columns(rows, w4),
            whole(rows, 256), pl.BlockSpec(memory_space=pl.ANY),
        ],
        [columns(rows, 512), leading(srows, 256)],
        [((rows, 2 * width), BF), ((groups * srows, 256), BF)],
        (attended_grad, rden, attended, phi_q, car, send),
        flops=1_000_000_000, moved=10_000_000,
    )
    sums, end = exchange(state_back, reach.T)
    query_grad, pk_local, vg_local = call(
        query_side_kernel, groups,
        [
            columns(rows, 512), columns(rows, 256), columns(rows, 256), columns(rows, w4),
            columns(rows, w4), leading(4, rows, rows), leading(srows, 256), leading(4, feats, 256),
            whole(rows, rows), whole(rows, 256),
        ],
        [columns(rows, 256), columns(rows, w4), columns(rows, 256)],
        [((rows, width), BF), ((rows, heads * feats), F32), ((rows, width), F32)],
        (ng, values, queries, phi_q, phi_k, scores, carry, pa, mask, car),
        flops=12_000_000_000, moved=30_000_000,
    )
    sums, query_grad, hidden_late, attn_late = lax.optimization_barrier(
        (sums, query_grad, hidden_grad, attn_grad)
    )
    later = end(sums)
    g_wo = dot_tn(attended, attn_late).astype(BF)
    g_wi = dot_tn(normed_bf, hidden_late).astype(BF)
    def side_by_side(value):
        return value.reshape(devices, share, -1)

    key_grad, value_grad = call(
        key_side_kernel, groups,
        [
            columns(rows, 256), columns(rows, 256), columns(rows, w4), leading(srows, 256),
            columns(rows, w4), columns(rows, 256), leading(4, feats, 256), whole(rows, 256),
        ],
        [columns(rows, 256), columns(rows, 256)],
        [((rows, width), BF), ((rows, width), BF)],
        (values, keys, phi_k, later, pk_local, vg_local, pa, las),
        flops=3_000_000_000, moved=12_000_000,
    )
    qkv_grad = jnp.concatenate([query_grad, key_grad, value_grad], axis=1)
    token_grad = first_grad + dot_nt(qkv_grad, all_one[:, : 3 * width])
    g_qkv = dot_tn(x, qkv_grad).astype(BF)
    column_grads = columns_of(
        [jnp.sum(qkv_grad[:, i * width : (i + 1) * width].astype(F32), axis=0) for i in range(3)]
        + [g_bo, g_ga, g_sa, g_bi, g_bu, g_gf, g_sf],
        devices,
    )

    late = [side_by_side(g) for g in (g_wo, g_wi, g_qkv)] + [column_grads.astype(BF)]
    chain = PairScatter(core_sums(late))
    chain.step()
    got_ffn = chain.after(got_ffn)
    while chain.orders[0]:
        chain.step()
    sizes = [v.shape[0] for v in first_vectors + rest_vectors]
    finals = finish_gradients(chain.held, got_ffn, share, width, early, parts, sizes)
    o_wq, o_wk, o_wv, o_wo, o_wi, o_wu = finals[:6]
    o_bq, o_bk, o_bv, o_bo, o_ga, o_sa, o_bi, o_bu, o_gf, o_sf = (v.reshape(-1) for v in finals[6:])
    return (
        output[None], token_grad[None], o_wq, o_bq, o_wk, o_bk, o_wv, o_bv, o_wo, o_bo,
        o_ga, o_sa, o_wi, o_bi, o_wu, o_bu, o_gf, o_sf,
    )


def solution(mesh):
    rows2 = P(("seq", "rep"), None)
    vec = P(("seq", "rep"))
    blocks = P("rep", "seq", None)
    in_specs = (
        blocks, P("rep", None), rows2, vec, rows2, vec, rows2, vec, rows2, vec, vec, vec,
        rows2, vec, rows2, vec, vec, vec, P(), blocks,
    )
    out_specs = (
        blocks, blocks, rows2, vec, rows2, vec, rows2, vec, rows2, vec, vec, vec,
        rows2, vec, rows2, vec, vec, vec,
    )
    return jax.shard_map(local, mesh=mesh, in_specs=in_specs, out_specs=out_specs, check_vma=False)
```

```python
import functools

import jax
import jax.numpy as jnp
from jax import lax
from jax.experimental import pallas as pl
from jax.experimental.pallas import tpu as pltpu
from jax.sharding import PartitionSpec as P

EPS = 1e-06
BF = jnp.bfloat16
F32 = jnp.float32
BOTH = ("seq", "rep")
VMEM_LIMIT = 50 * 1024 * 1024
STATE_ROWS = 16


def dot(a, b):
    return lax.dot_general(a, b, (((1,), (0,)), ((), ())), preferred_element_type=F32)


def dot_nt(a, b):
    return lax.dot_general(a, b, (((1,), (1,)), ((), ())), preferred_element_type=F32)


def dot_tn(a, b):
    return lax.dot_general(a, b, (((0,), (0,)), ((), ())), preferred_element_type=F32)


def half_masks(rows):
    lane = lax.broadcasted_iota(jnp.int32, (rows, 128), 1)
    return (lane < 64, lane >= 64)


def with_ones(values_pair, mask):
    zero = jnp.zeros_like(values_pair)
    return jnp.concatenate(
        [jnp.where(mask, values_pair, zero), jnp.where(mask, zero + 1, zero)], axis=1
    )


def state_matrix(state_ref, head, side, spread):
    state = state_ref[head * 64 : (head + 1) * 64, :]
    norm = state_ref[256:272, :][head : head + 1, :]
    zero = jnp.zeros((64, 256), BF)
    if spread:
        norm_rows = jnp.broadcast_to(norm, (64, 256))
    else:
        row = lax.broadcasted_iota(jnp.int32, (64, 256), 0)
        norm_rows = jnp.where(row == 0, jnp.broadcast_to(norm, (64, 256)), zero)
    if side == 0:
        return jnp.concatenate([state, zero, norm_rows, zero], axis=0)
    return jnp.concatenate([zero, state, zero, norm_rows], axis=0)


def features(rows_bf, squares, mask, padded):
    scale = 64 ** (-0.25)
    square = jnp.sum(jnp.where(mask, squares, 0.0), axis=1, keepdims=True)
    return (jnp.exp(scale * dot(rows_bf, padded) - square * 0.0625) * 0.0625).astype(BF)


def keys_kernel(
    x_ref, wk_ref, wv_ref, bk_ref, bv_ref, pp_ref, last_ref, k_ref, v_ref, phik_ref, st_ref
):
    x = x_ref[...]
    k_ref[...] = (dot(x, wk_ref[...]) + bk_ref[...]).astype(BF)
    v_ref[...] = (dot(x, wv_ref[...]) + bv_ref[...]).astype(BF)
    masks = half_masks(x.shape[0])
    norms = []
    for pair in range(2):
        lanes = slice(pair * 128, (pair + 1) * 128)
        kp = k_ref[:, lanes]
        vp = v_ref[:, lanes]
        k2 = kp.astype(F32) * kp.astype(F32)
        for side in range(2):
            head = 2 * pair + side
            phi_k = features(kp, k2, masks[side], pp_ref[head])
            phik_ref[:, head * 256 : (head + 1) * 256] = phi_k
            state = dot_tn(with_ones(vp, masks[side]), phi_k * last_ref[...])
            st_ref[head * 64 : (head + 1) * 64, :] = state[side * 64 : (side + 1) * 64].astype(BF)
            norms.append(state[128 + side * 64 : 129 + side * 64])
    norms.append(jnp.zeros((STATE_ROWS - 4, 256), F32))
    st_ref[256:272, :] = jnp.concatenate(norms, axis=0).astype(BF)


def queries_kernel(
    x_ref, wq_ref, bq_ref, v_ref, phik_ref, pp_ref, mask_ref, q_ref, phiq_ref, s_ref, nd_ref
):
    x = x_ref[...]
    rows = x.shape[0]
    half = rows // 2
    q_ref[...] = (dot(x, wq_ref[...]) + bq_ref[...]).astype(BF)
    masks = half_masks(rows)
    for pair in range(2):
        lanes = slice(pair * 128, (pair + 1) * 128)
        qp = q_ref[:, lanes]
        vp = v_ref[:, lanes]
        q2 = qp.astype(F32) * qp.astype(F32)
        top = jnp.zeros((half, 256), F32)
        bottom = jnp.zeros((half, 256), F32)
        for side in range(2):
            head = 2 * pair + side
            cols = slice(head * 256, (head + 1) * 256)
            phi_q = features(qp, q2, masks[side], pp_ref[head])
            phi_k = phik_ref[:, cols]
            phiq_ref[:, cols] = phi_q
            va = with_ones(vp, masks[side])
            s_top = (dot_nt(phi_q[:half], phi_k[:half]) * mask_ref[:half, :half]).astype(BF)
            s_bot = (dot_nt(phi_q[half:], phi_k) * mask_ref[half:, :]).astype(BF)
            s_ref[head, :half, :half] = s_top
            s_ref[head, half:, :] = s_bot
            top = top + dot(s_top, va[:half])
            bottom = bottom + dot(s_bot, va)
        nd_ref[:half, pair * 256 : (pair + 1) * 256] = top
        nd_ref[half:, pair * 256 : (pair + 1) * 256] = bottom


def finish_kernel(phiq_ref, nd_ref, cs_ref, car_ref, att_ref, rden_ref):
    car = car_ref[...]
    for pair in range(2):
        nd = nd_ref[:, pair * 256 : (pair + 1) * 256]
        for side in range(2):
            head = 2 * pair + side
            phi_q = phiq_ref[:, head * 256 : (head + 1) * 256] * car
            nd = nd + dot_nt(phi_q, state_matrix(cs_ref, head, side, True))
        rden = 1.0 / nd[:, 128:]
        lanes = slice(pair * 128, (pair + 1) * 128)
        att_ref[:, lanes] = (nd[:, :128] * rden).astype(BF)
        rden_ref[:, lanes] = rden


def state_grad_kernel(ag_ref, rden_ref, att_ref, phiq_ref, car_ref, _send, ng_ref, sg_ref):
    car = car_ref[...]
    norms = []
    for pair in range(2):
        lanes = slice(pair * 128, (pair + 1) * 128)
        ng = ag_ref[:, lanes] * rden_ref[:, lanes]
        dg = -(ng * att_ref[:, lanes].astype(F32))
        both = jnp.concatenate([ng.astype(BF), dg.astype(BF)], axis=1)
        ng_ref[:, pair * 256 : (pair + 1) * 256] = both
        both = both * car
        for side in range(2):
            head = 2 * pair + side
            state = dot_tn(both, phiq_ref[:, head * 256 : (head + 1) * 256])
            sg_ref[head * 64 : (head + 1) * 64, :] = state[side * 64 : (side + 1) * 64].astype(BF)
            tail = state[128 + side * 64 : 192 + side * 64]
            norms.append(jnp.sum(tail, axis=0, keepdims=True))
    norms.append(jnp.zeros((STATE_ROWS - 4, 256), F32))
    sg_ref[256:272, :] = jnp.concatenate(norms, axis=0).astype(BF)


def column_sums(value, lane):
    lanes = lax.broadcasted_iota(jnp.int32, (value.shape[0], 128), 1)
    one = jnp.ones((value.shape[0], 128), BF)
    return dot_tn(value, jnp.where(lanes == lane, one, jnp.zeros_like(one)))


def query_side_kernel(
    ng_ref, v_ref, q_ref, phiq_ref, phik_ref, s_ref, cs_ref, pa_ref, mask_ref, car_ref,
    qg_ref, pk_ref, vg_ref, bq_ref,
):
    rows = q_ref.shape[0]
    half = rows // 2
    scale = 64 ** (-0.25)
    masks = half_masks(rows)
    car = car_ref[...]
    for pair in range(2):
        lanes = slice(pair * 128, (pair + 1) * 128)
        both = ng_ref[:, pair * 256 : (pair + 1) * 256]
        both_car = both * car
        vp = v_ref[:, lanes]
        ng = both[:, :128]
        out_q = jnp.zeros((rows, 256), F32)
        vg_top = jnp.zeros((half, 128), F32)
        vg_bot = jnp.zeros((half, 128), F32)
        for side in range(2):
            head = 2 * pair + side
            cols = slice(head * 256, (head + 1) * 256)
            va = with_ones(vp, masks[side])
            phi_q = phiq_ref[:, cols]
            phi_k = phik_ref[:, cols]
            g_top = (dot_nt(both[:half], va[:half]) * mask_ref[:half, :half]).astype(BF)
            g_bot = (dot_nt(both[half:], va) * mask_ref[half:, :]).astype(BF)
            carry = dot(both_car, state_matrix(cs_ref, head, side, True))
            pq_top = dot(g_top, phi_k[:half]) + carry[:half]
            pq_bot = dot(g_bot, phi_k) + carry[half:]
            pq = jnp.concatenate([pq_top, pq_bot], axis=0)
            iq = (scale * (pq * phi_q.astype(F32))).astype(BF)
            out_q = out_q + dot(iq, pa_ref[head])
            pk = dot_tn(g_bot, phi_q[half:])
            pk_ref[half:, cols] = pk[half:].astype(BF)
            pk_ref[:half, cols] = (pk[:half] + dot_tn(g_top, phi_q[:half])).astype(BF)
            ngm = jnp.where(masks[side], ng, jnp.zeros_like(ng))
            s_bot = s_ref[head, half:, :]
            s_top = s_ref[head, :half, :half]
            from_bot = dot_tn(s_bot, ngm[half:])
            vg_bot = vg_bot + from_bot[half:]
            vg_top = vg_top + from_bot[:half] + dot_tn(s_top, ngm[:half])
        qp = q_ref[:, lanes].astype(F32)
        qg = (out_q[:, :128] - scale * qp * out_q[:, 128:]).astype(BF)
        qg_ref[:, lanes] = qg
        bq_ref[lanes, :] = column_sums(qg, 0)
        vg_ref[:half, lanes] = vg_top
        vg_ref[half:, lanes] = vg_bot


def key_side_kernel(
    v_ref, k_ref, phik_ref, ls_ref, pk_ref, vgl_ref, pa_ref, last_ref,
    others_ref, bq_ref, kg_ref, vg_ref, vectors_ref,
):
    rows = k_ref.shape[0]
    scale = 64 ** (-0.25)
    masks = half_masks(rows)
    last = last_ref[...]
    for pair in range(2):
        lanes = slice(pair * 128, (pair + 1) * 128)
        vp = v_ref[:, lanes]
        out_k = jnp.zeros((rows, 256), F32)
        vg = vgl_ref[:, lanes]
        for side in range(2):
            head = 2 * pair + side
            cols = slice(head * 256, (head + 1) * 256)
            va = with_ones(vp, masks[side]) * last
            phi_k = phik_ref[:, cols]
            later = state_matrix(ls_ref, head, side, False)
            pk = pk_ref[:, cols].astype(F32) + dot(va, later)
            ik = (scale * (pk * phi_k.astype(F32))).astype(BF)
            out_k = out_k + dot(ik, pa_ref[head])
            vg = vg + dot_nt(phi_k * last, later[:128])
        kp = k_ref[:, lanes].astype(F32)
        kg = (out_k[:, :128] - scale * kp * out_k[:, 128:]).astype(BF)
        vg = vg.astype(BF)
        kg_ref[:, lanes] = kg
        vg_ref[:, lanes] = vg
        total = others_ref[lanes, :] + bq_ref[lanes, :]
        total = total + column_sums(kg, 1) + column_sums(vg, 2)
        vectors_ref[lanes, :] = total.astype(BF)


def columns(rows, width, first=0):
    return pl.BlockSpec((rows, width), lambda g: (0, g + first))


def whole(*shape):
    return pl.BlockSpec(shape, lambda g: (0,) * len(shape))


def leading(count, *rest):
    return pl.BlockSpec((count,) + rest, lambda g: (g,) + (0,) * len(rest))


def call(kernel, groups, in_specs, out_specs, outs, args, flops=0, moved=0):
    return pl.pallas_call(
        kernel,
        grid=(groups,),
        in_specs=in_specs,
        out_specs=out_specs,
        out_shape=[jax.ShapeDtypeStruct(shape, kind) for shape, kind in outs],
        compiler_params=pltpu.CompilerParams(vmem_limit_bytes=VMEM_LIMIT),
        cost_estimate=pl.CostEstimate(flops=flops, bytes_accessed=moved, transcendentals=0),
    )(*args)


def exchange(state, matrix):
    count = lax.axis_size("seq")
    rows, width = state.shape
    extra = -rows % count
    if extra:
        state = jnp.pad(state, ((0, extra), (0, 0)))
    parts = state.reshape(count, (rows + extra) // count, width)
    parts = lax.all_to_all(parts, "seq", 0, 0)
    summed = jnp.einsum("cb,bre->cre", matrix.astype(BF), parts, preferred_element_type=F32)

    def end(sums):
        back = lax.all_to_all(sums, "seq", 0, 0)
        return back.reshape(rows + extra, width)[:rows]

    return summed.astype(BF), end


def device_bits():
    count = lax.axis_size("seq") * lax.axis_size("rep")
    bits = count.bit_length() - 1
    assert count == 1 << bits and bits >= 3
    return count, bits, lax.axis_index("seq") * lax.axis_size("rep") + lax.axis_index("rep")


def swap(value, bit):
    count, _, _ = device_bits()
    return lax.ppermute(value, BOTH, [(i, i ^ (1 << bit)) for i in range(count)])


def stage_orders(bits, ways):
    order = list(range(1, bits))
    turned = min(ways, bits - 1)
    return [order[k:turned] + order[:k] + order[turned:] for k in range(turned)]


def gather_pairs(block):
    _, bits, me = device_bits()
    rows, width = block.shape

    def grow(held, bit, axis):
        other = swap(held, bit)
        low = (me >> bit) & 1 == 0
        return jnp.stack([jnp.where(low, held, other), jnp.where(low, other, held)], axis=axis)

    orders = [order[::-1] for order in stage_orders(bits, 3)]
    tiles = width // 128
    cuts = [tiles * k // len(orders) * 128 for k in range(len(orders) + 1)]
    parts = [block[:, cuts[k] : cuts[k + 1]] for k in range(len(orders))]
    have = [[] for _ in orders]
    if len({order[0] for order in orders}) == 1:
        shared = orders[0][0]
        grown = grow(block, shared, 0)
        parts = [grown[:, :, cuts[k] : cuts[k + 1]] for k in range(len(orders))]
        have = [[shared] for _ in orders]
        orders = [order[1:] for order in orders]
    for stage in range(len(orders[0])):
        for k, order in enumerate(orders):
            bit = order[stage]
            axis = sum(b > bit for b in have[k])
            have[k].append(bit)
            parts[k] = grow(parts[k], bit, axis)
    parts = [part.reshape((-1,) + part.shape[-2:]) for part in parts]
    return grow(jnp.concatenate(parts, axis=2), 0, 1).reshape(-1, width)


def add(mine, other):
    return (mine.astype(F32) + other.astype(F32)).astype(BF)


def pick(me, value, bit, axis, own):
    index = (me >> bit) & 1
    return lax.dynamic_index_in_dim(value, index if own else 1 - index, axis, False)


def core_sums(pieces):
    count, _, _ = device_bits()
    cores = lax.axis_size("rep")
    pairs = [piece.reshape(count // 2, 2, -1, piece.shape[-1]).swapaxes(0, 1) for piece in pieces]
    both = jnp.concatenate(pairs, axis=3)
    groups = [[core, core + 1] for core in range(0, cores, 2)]
    both = lax.all_to_all(both, "rep", 0, 0, axis_index_groups=groups)
    return add(both[0], both[1])


class PairScatter:
    def __init__(self, value):
        _, self.bits, self.me = device_bits()
        self.orders = stage_orders(self.bits, 3)
        turned = len(self.orders)
        self.left = [list(range(self.bits - 1, 0, -1)) for _ in self.orders]
        tiles = value.shape[2] // 128
        cuts = [tiles * k // turned * 128 for k in range(turned + 1)]
        value = value.reshape((2,) * (self.bits - 1) + value.shape[1:])
        self.held = [value[..., cuts[k] : cuts[k + 1]] for k in range(turned)]

    def step(self):
        for k, order in enumerate(self.orders):
            bit, self.orders[k] = order[0], order[1:]
            axis = self.left[k].index(bit)
            self.left[k].remove(bit)
            held = self.held[k]
            moved = swap(pick(self.me, held, bit, axis, False), bit)
            self.held[k] = add(pick(self.me, held, bit, axis, True), moved)

    def after(self, value):
        self.me, value = lax.optimization_barrier((self.me, value))
        return value


def columns_of(vectors, count):
    rows = min(v.size for v in vectors) // count
    found = [jnp.swapaxes(v.reshape(count, -1, rows), 1, 2) for v in vectors]
    found = jnp.concatenate(found, axis=2)
    return jnp.pad(found, ((0, 0), (0, 0), (0, 128 - found.shape[2])))


def vectors_of(block, sizes, count):
    rows = block.shape[0] // count
    found = []
    at = 0
    for size in sizes:
        lanes = size // rows
        item = block[:, at : at + lanes].reshape(count, rows, lanes)
        found.append(jnp.swapaxes(item, 1, 2).reshape(1, -1).astype(F32))
        at += lanes
    return found


def finish_gradients(held, got_ffn, share, width, early, parts, sizes):
    late = (parts - early) * width
    shapes = [(share, width)] * 4 + [(share, parts * width), (parts * share, width)]
    shapes += [(size // share, share) for size in sizes]

    def pieces(got, ffn, turn):
        at = width + late
        found = [got[:, at + k * width : at + (k + 1) * width] for k in range(3)] + [got[:, :width]]
        early_parts = [ffn[k * share : (k + 1) * share] for k in range(early)]
        found.append(jnp.concatenate(early_parts + [got[:, width:at]], axis=1))
        found.append(ffn[early * share :])
        turned = turn(got[:, at + 3 * width :])
        row = 0
        for size in sizes:
            found.append(turned[row : row + size // share])
            row += size // share
        return found

    if share % 8:
        got = jnp.concatenate(held, axis=1).astype(F32)
        return pieces(got, got_ffn.astype(F32), jnp.transpose)

    def kernel(*refs):
        count = len(held)
        got = jnp.concatenate([ref[...].astype(F32) for ref in refs[:count]], axis=1)
        for ref, value in zip(refs[count + 1 :], pieces(got, refs[count][...].astype(F32), jnp.transpose)):
            ref[...] = value

    return pl.pallas_call(
        kernel,
        out_shape=[jax.ShapeDtypeStruct(shape, F32) for shape in shapes],
        compiler_params=pltpu.CompilerParams(vmem_limit_bytes=VMEM_LIMIT),
        cost_estimate=pl.CostEstimate(flops=1000, bytes_accessed=2_000_000, transcendentals=0),
    )(*held, got_ffn)


def norm_rows(value):
    centre = jnp.mean(value, axis=-1, keepdims=True)
    centred = value - centre
    spread = jnp.mean(centred * centred, axis=-1, keepdims=True)
    inverse = lax.rsqrt(spread + EPS)
    return centred * inverse, inverse


def norm_back(grad, gain, unit, inverse):
    scaled = grad * gain
    mean_one = jnp.mean(scaled, axis=-1, keepdims=True)
    mean_two = jnp.mean(scaled * unit, axis=-1, keepdims=True)
    return (scaled - mean_one - unit * mean_two) * inverse


def local(
    tokens, lengths, w_query, b_query, w_key, b_key, w_value, b_value, w_out, b_out,
    gain_attn, shift_attn, w_inner, b_inner, w_outer, b_outer, gain_ffn, shift_ffn,
    projection, cotangent,
):
    rows = tokens.shape[1]
    width = tokens.shape[2]
    heads = projection.shape[0]
    feats = projection.shape[1]
    groups = heads // 4
    blocks = lax.axis_size("seq")
    devices = blocks * lax.axis_size("rep")
    here = lax.axis_index("seq")
    share = w_query.shape[0]
    hidden_width = w_inner.shape[1]
    parts = hidden_width // width

    first_vectors = (b_query, b_key, b_value)
    rest_vectors = (b_out, gain_attn, shift_attn, b_inner, b_outer, gain_ffn, shift_ffn)
    pack_one = jnp.concatenate([w_query, w_key, w_value, w_out, columns_of(first_vectors, 1)[0]], axis=1)
    pack_two = jnp.concatenate([w_inner, columns_of(rest_vectors, 1)[0]], axis=1)
    all_two = lax.all_gather(pack_two, BOTH, axis=0, tiled=True)
    w_ou = lax.all_gather(w_outer, BOTH, axis=0, tiled=True)
    all_one = gather_pairs(pack_one)
    bq, bk, bv = vectors_of(all_one[:, 4 * width :], [v.shape[0] for v in first_vectors], devices)
    wo = all_one[:, 3 * width : 4 * width]
    w_in = all_two[:, :hidden_width]
    bo, ga, sa, bi, bu, gf, sf = vectors_of(
        all_two[:, hidden_width:], [v.shape[0] for v in rest_vectors], devices
    )

    def shares(value):
        return value.reshape(devices, -1, width)

    sizes = lengths[0]
    starts = jnp.cumsum(sizes) - sizes

    def begin_of(places):
        below = starts[None, :] <= places[:, None]
        begins = jnp.max(jnp.where(below, starts[None, :], -1), axis=1)
        return begins, jnp.sum(below.astype(jnp.int32), axis=1) - 1

    offset = here * rows
    places = offset + jnp.arange(rows, dtype=jnp.int32)
    begins, docs = begin_of(places)
    carried = (begins < offset).astype(BF)
    last = (docs == docs[-1]).astype(BF)
    causal = (docs[:, None] == docs[None, :]) & (places[None, :] <= places[:, None])
    mask = causal.astype(F32)
    car = jnp.broadcast_to(carried[:, None], (rows, 256))
    las = jnp.broadcast_to(last[:, None], (rows, 256))
    block = jnp.arange(blocks, dtype=jnp.int32)
    end_begin, _ = begin_of(block * rows + rows - 1)
    flags = (end_begin >= block * rows).astype(jnp.int32)
    before = jnp.cumsum(flags) - flags
    reach = (block[:, None] > block[None, :]) & (
        before[:, None] - before[None, :] - flags[None, :] == 0
    )
    reach = reach.astype(BF)

    pairs = projection.reshape(heads // 2, 2, feats, 64)
    first = jnp.pad(pairs[:, 0], ((0, 0), (0, 0), (0, 64)))
    second = jnp.pad(pairs[:, 1], ((0, 0), (0, 0), (64, 0)))
    padded = jnp.stack([first, second], axis=1).reshape(heads, feats, 128)
    lane = jnp.arange(128)
    lane_ones = jnp.stack([lane < 64, lane >= 64]).astype(BF)
    lane_ones = jnp.broadcast_to(lane_ones[None, :, None, :], (heads // 2, 2, feats, 128))
    pa = jnp.concatenate([padded, lane_ones.reshape(heads, feats, 128)], axis=-1)
    pp = jnp.swapaxes(padded, 1, 2)

    x = tokens[0]
    srows = 256 + STATE_ROWS
    w4 = 4 * feats
    keys, values, phi_k, state = call(
        keys_kernel, groups,
        [
            whole(rows, width), columns(width, 256, groups), columns(width, 256, 2 * groups),
            columns(1, 256), columns(1, 256), leading(4, 128, feats), whole(rows, 256),
        ],
        [columns(rows, 256), columns(rows, 256), columns(rows, w4), leading(srows, 256)],
        [
            ((rows, width), BF), ((rows, width), BF), ((rows, heads * feats), BF),
            ((groups * srows, 256), BF),
        ],
        (x, all_one, all_one, bk, bv, pp, las),
        flops=4_000_000_000, moved=9_000_000,
    )
    sums, end = exchange(state, reach)
    queries, phi_q, scores, nd = call(
        queries_kernel, groups,
        [
            whole(rows, width), columns(width, 256), columns(1, 256), columns(rows, 256),
            columns(rows, w4), leading(4, 128, feats), whole(rows, rows),
        ],
        [columns(rows, 256), columns(rows, w4), leading(4, rows, rows), columns(rows, 512)],
        [
            ((rows, width), BF), ((rows, heads * feats), BF), ((heads, rows, rows), BF),
            ((rows, 2 * width), F32),
        ],
        (x, all_one, bq, values, phi_k, pp, mask),
        flops=8_000_000_000, moved=20_000_000,
    )
    sums, nd = lax.optimization_barrier((sums, nd))
    carry = end(sums)
    attended, rden = call(
        finish_kernel, groups,
        [columns(rows, w4), columns(rows, 512), leading(srows, 256), whole(rows, 256)],
        [columns(rows, 256), columns(rows, 256)],
        [((rows, width), BF), ((rows, width), F32)],
        (phi_q, nd, carry, car),
        flops=1_000_000_000, moved=10_000_000,
    )

    xf = x.astype(F32)
    unit_one, inv_one = norm_rows(xf + dot(attended, wo) + bo)
    normed = unit_one * ga + sa
    normed_bf = normed.astype(BF)
    hidden = dot(normed_bf, w_in) + bi
    cdf = 0.5 * (1.0 + lax.erf(hidden * (0.5**0.5)))
    activated = (hidden * cdf).astype(BF)
    ffn = dot(activated, w_ou) + bu
    unit_two, inv_two = norm_rows(normed + ffn)
    output = (unit_two * gf + sf).astype(BF)

    upstream = cotangent[0].astype(F32)
    sum_grad = norm_back(upstream, gf, unit_two, inv_two)
    g_gf = jnp.sum(upstream * unit_two, axis=0)
    g_sf = jnp.sum(upstream, axis=0)
    ffn_grad = sum_grad.astype(BF)
    g_bu = jnp.sum(ffn_grad.astype(F32), axis=0)
    g_wu = dot_tn(activated, ffn_grad).astype(BF)
    density = jnp.exp(-0.5 * hidden * hidden) * 0.3989422804014327
    hidden_grad = (dot_nt(ffn_grad, w_ou) * (cdf + hidden * density)).astype(BF)
    g_bi = jnp.sum(hidden_grad.astype(F32), axis=0)

    send = shares(g_wu)
    early = 0
    got_ffn = lax.psum_scatter(send, BOTH, scatter_dimension=0, tiled=False)
    normed_grad = sum_grad + dot_nt(hidden_grad, w_in)
    first_grad = norm_back(normed_grad, ga, unit_one, inv_one)
    g_ga = jnp.sum(normed_grad * unit_one, axis=0)
    g_sa = jnp.sum(normed_grad, axis=0)
    attn_grad = first_grad.astype(BF)
    g_bo = jnp.sum(attn_grad.astype(F32), axis=0)
    attended_grad = dot_nt(attn_grad, wo)

    ng, state_back = call(
        state_grad_kernel, groups,
        [
            columns(rows, 256), columns(rows, 256), columns(rows, 256), columns(rows, w4),
            whole(rows, 256), pl.BlockSpec(memory_space=pl.ANY),
        ],
        [columns(rows, 512), leading(srows, 256)],
        [((rows, 2 * width), BF), ((groups * srows, 256), BF)],
        (attended_grad, rden, attended, phi_q, car, send),
        flops=1_000_000_000, moved=10_000_000,
    )
    sums, end = exchange(state_back, reach.T)
    query_grad, pk_local, vg_local, sum_q = call(
        query_side_kernel, groups,
        [
            columns(rows, 512), columns(rows, 256), columns(rows, 256), columns(rows, w4),
            columns(rows, w4), leading(4, rows, rows), leading(srows, 256), leading(4, feats, 256),
            whole(rows, rows), whole(rows, 256),
        ],
        [columns(rows, 256), columns(rows, w4), columns(rows, 256), leading(256, 128)],
        [
            ((rows, width), BF), ((rows, heads * feats), BF), ((rows, width), F32),
            ((width, 128), F32),
        ],
        (ng, values, queries, phi_q, phi_k, scores, carry, pa, mask, car),
        flops=12_000_000_000, moved=30_000_000,
    )
    sums, query_grad, hidden_late, attn_late = lax.optimization_barrier(
        (sums, query_grad, hidden_grad, attn_grad)
    )
    later = end(sums)
    g_wo = dot_tn(attended, attn_late).astype(BF)
    g_wi = dot_tn(normed_bf, hidden_late).astype(BF)
    def side_by_side(value):
        return value.reshape(devices, share, -1)

    nothing = jnp.zeros((width,), F32)
    others = columns_of([nothing] * 3 + [g_bo, g_ga, g_sa, g_bi, g_bu, g_gf, g_sf], devices)
    key_grad, value_grad, column_grads = call(
        key_side_kernel, groups,
        [
            columns(rows, 256), columns(rows, 256), columns(rows, w4), leading(srows, 256),
            columns(rows, w4), columns(rows, 256), leading(4, feats, 256), whole(rows, 256),
            leading(256, 128), leading(256, 128),
        ],
        [columns(rows, 256), columns(rows, 256), leading(256, 128)],
        [((rows, width), BF), ((rows, width), BF), ((width, 128), BF)],
        (
            values, keys, phi_k, later, pk_local, vg_local, pa, las,
            others.reshape(width, 128), sum_q,
        ),
        flops=3_000_000_000, moved=12_000_000,
    )
    qkv_grad = jnp.concatenate([query_grad, key_grad, value_grad], axis=1)
    token_grad = first_grad + dot_nt(qkv_grad, all_one[:, : 3 * width])
    g_qkv = dot_tn(x, qkv_grad).astype(BF)
    late = [side_by_side(g) for g in (g_wo, g_wi, g_qkv, column_grads)]
    chain = PairScatter(core_sums(late))
    chain.step()
    got_ffn = chain.after(got_ffn)
    while chain.orders[0]:
        chain.step()
    sizes = [v.shape[0] for v in first_vectors + rest_vectors]
    finals = finish_gradients(chain.held, got_ffn, share, width, early, parts, sizes)
    o_wq, o_wk, o_wv, o_wo, o_wi, o_wu = finals[:6]
    o_bq, o_bk, o_bv, o_bo, o_ga, o_sa, o_bi, o_bu, o_gf, o_sf = (v.reshape(-1) for v in finals[6:])
    return (
        output[None], token_grad[None], o_wq, o_bq, o_wk, o_bk, o_wv, o_bv, o_wo, o_bo,
        o_ga, o_sa, o_wi, o_bi, o_wu, o_bu, o_gf, o_sf,
    )


def solution(mesh):
    rows2 = P(("seq", "rep"), None)
    vec = P(("seq", "rep"))
    blocks = P("rep", "seq", None)
    in_specs = (
        blocks, P("rep", None), rows2, vec, rows2, vec, rows2, vec, rows2, vec, vec, vec,
        rows2, vec, rows2, vec, vec, vec, P(), blocks,
    )
    out_specs = (
        blocks, blocks, rows2, vec, rows2, vec, rows2, vec, rows2, vec, vec, vec,
        rows2, vec, rows2, vec, vec, vec,
    )
    return jax.shard_map(local, mesh=mesh, in_specs=in_specs, out_specs=out_specs, check_vma=False)
```
